32 devices in a mesh: shot: 2 (over y), gy: 4 (over z), freq: 2 (over x), fld: 2 (over core).
Axes of the slice: x: 2, y: 2, z: 4, core: 2. Of those that a mesh axis runs over, the one named last changes fastest.
Arguments:
- wavefields: float32 [2, 2, 8, 1024, 1024], P('fld', None, ('shot', 'freq'), 'gy'), parts along dimension 2, may hold values from -6 to 6
- slowness: float32 [2, 1024, 1024], P(None, 'gy'), may hold values from 0.7 to 1.3
- freq_index: int32 [4], P('freq'), may hold values from 15 to 27
Outputs:
- image: float32 [4, 1024, 1024], P('shot', 'gy', ('freq', 'fld')), parts along dimension 0
The draws below stay inside these ranges and needn't reach their ends.
There are 2 independent parts, one for each index of `shot`. The reference program is written for one: setup_inputs(seed, part) draws one part's arguments, and reference() takes and returns one part's arrays. A program takes and returns all parts, laid end to end along the dimension named above; an argument that names none is the same for every part. Nothing has to cross between parts.
Inputs may be any that keep to these rules, and one draw needn't show every extreme that they name: `freq_index`: frequency index k stands for the angular frequency 0.1 k.
All inputs are finite; a program needn't handle non-finite values.
Results may differ from the reference program's by a relative error of at most 0.0003.
Values sent between devices are 32-bit elements; how exact they have to be, the bound alone decides.
No kernel may reach another device: no remote copies, remote signals or barrier semaphores. Data moves between devices by JAX's collectives and lax.ppermute only.
A program may use at most 64 MiB of HBM per device.

```python
import math
import jax
import jax.numpy as jnp
from jax import lax

NX = 1024
NY = 1024
DEPTH = 2
F = 4


def with_ends(array, own_key, smallest, high):
    index_at = [jax.random.randint(jax.random.fold_in(own_key, axis), (), 0, length) for axis, length in enumerate(array.shape)]
    main_axis = array.shape.index(max(array.shape))
    neighbour = index_at[:main_axis] + [(index_at[main_axis] + 1) % array.shape[main_axis]] + index_at[main_axis + 1:]
    return array.at[tuple(index_at)].set(smallest).at[tuple(neighbour)].set(high)


def steps_of(own_key, dims, cuts, smallest, top_value):
    gain = 1.0
    for position, blocks in cuts:
        steps = jax.random.uniform(jax.random.fold_in(jax.random.fold_in(own_key, 6), position), (blocks,), jnp.float32, smallest / len(cuts), top_value / len(cuts))
        gain = gain * jnp.repeat(jnp.exp(steps), dims[position] // blocks).reshape((-1,) + (1,) * (len(dims) - 1 - position))
    return gain


def centred(key, dims, deviation, most, shards=(), held_as=jnp.bfloat16):
    entries = jax.random.normal(key, dims, jnp.float32) * deviation
    if len(shards) > 0:
        entries = steps_of(key, dims, shards, -0.22, 0.18) * entries
    return jnp.clip(entries, min=-most, max=most).astype(held_as)


def setup_inputs(seed: int = 0, part: int = 0) -> dict:
    streams_of = jax.random.split(jax.random.key(seed), 4)
    part_splits = jax.random.split(jax.random.fold_in(streams_of[3], part), 4)
    wavefields = centred(part_splits[0], (2, 2, F, NX, NY), 1.0, 6.0, ((0, 2), (2, 2), (3, 4)), jnp.float32)
    slowness = jnp.clip(0.7 + 0.59999996 * jax.random.uniform(streams_of[1], (DEPTH, NX, NY), jnp.float32) ** steps_of(streams_of[1], (DEPTH, NX, NY), ((1, 4),), -0.2, 0.2), 0.7, 1.3)
    freq_index = with_ends(jax.random.randint(streams_of[2], (F,), 15, 28), jax.random.fold_in(streams_of[2], 1), 15, 27).astype(jnp.int32)
    return dict(wavefields=wavefields, slowness=slowness, freq_index=freq_index)


omega_unit = 0.1
reference_slowness = 1.0
depth_interval = 1.0

def wave_number(length):
    indices = jnp.arange(length, dtype=jnp.int32)
    signed = jnp.where(indices < length // 2, indices, indices - length)
    return 2.0 * math.pi / length * signed.astype(jnp.float32)

def one_step(wavefield, omega_now, polarity, screen, kz_square):
    spectrum = jnp.fft.fft2(wavefield)
    kz_root = jnp.sqrt(jnp.abs(kz_square))
    travels = kz_square >= 0.0
    amplitude = jnp.where(travels, 1.0, jnp.exp(-kz_root * depth_interval))
    angles = jnp.where(travels, polarity * kz_root * depth_interval, 0.0)
    spectrum = spectrum * lax.complex(amplitude * jnp.cos(angles), amplitude * jnp.sin(angles))
    wavefield = jnp.fft.ifft2(spectrum)
    phases = polarity * omega_now * (screen - reference_slowness) * depth_interval
    return wavefield * lax.complex(jnp.cos(phases), jnp.sin(phases))

def reference(wavefields, slowness, freq_index):
    x_waves = wave_number(NX)
    y_waves = wave_number(NY)
    lateral = x_waves[:, None] ** 2 + y_waves[None, :] ** 2
    stacked = jnp.moveaxis(wavefields, 2, 0)

    def accumulate(images, inputs):
        fields, freq_now = inputs
        omega_now = omega_unit * freq_now.astype(jnp.float32)
        kz_square = (omega_now * reference_slowness) ** 2 - lateral
        source = lax.complex(fields[0, 0], fields[0, 1])
        receiver = lax.complex(fields[1, 0], fields[1, 1])
        term_list = []
        for depth_step in range(DEPTH):
            source = one_step(source, omega_now, -1.0, slowness[depth_step], kz_square)
            receiver = one_step(receiver, omega_now, 1.0, slowness[depth_step], kz_square)
            term_list.append(jnp.real(source) * jnp.real(receiver) + jnp.imag(source) * jnp.imag(receiver))
        return (images + jnp.stack(term_list), None)
    images, unused = lax.scan(accumulate, jnp.zeros((DEPTH, NX, NY), jnp.float32), (stacked, freq_index))
    return images
```

```python
import functools
import math

import jax
import jax.numpy as jnp
import numpy as np
from jax import lax
from jax.experimental import pallas as pl
from jax.experimental.pallas import tpu as pltpu
from jax.sharding import PartitionSpec as P

DEPTH = 2


omega_unit = 0.1
reference_slowness = 1.0
depth_interval = 1.0
inner_length = 128


def contract(pattern, values, matrix):
    return jnp.einsum(
        pattern, values, matrix, precision=lax.Precision.HIGHEST, preferred_element_type=jnp.float32
    )


def complex_table(length, polarity):
    indices = jnp.arange(length, dtype=jnp.int32)
    angles = (
        2.0 * math.pi / length * (indices[:, None] * indices[None, :] % length).astype(jnp.float32)
    )
    cosine = jnp.cos(angles)
    sine_part = polarity * jnp.sin(angles)
    upper = jnp.stack([cosine, sine_part], axis=1)
    lower = jnp.stack([-sine_part, cosine], axis=1)
    return jnp.stack([upper, lower], axis=0)


def twiddle(outer_size, inner_size, length, polarity):
    outer_index = jnp.arange(outer_size, dtype=jnp.int32)[:, None]
    inner_index = jnp.arange(inner_size, dtype=jnp.int32)[None, :]
    angles = 2.0 * math.pi / length * (outer_index * inner_index % length).astype(jnp.float32)
    return (jnp.cos(angles), polarity * jnp.sin(angles))


def rotate(values, cosine, sine_part):
    real_part = values[0]
    imag_part = values[1]
    return jnp.stack(
        [real_part * cosine - imag_part * sine_part, real_part * sine_part + imag_part * cosine]
    )


def wave_number(indices, length):
    signed = jnp.where(indices < length // 2, indices, indices - length)
    return 2.0 * math.pi / length * signed.astype(jnp.float32)


def forward_rows(wave_field):
    batches, x_rows, y_cols = wave_field.shape[1:]
    outer_size = y_cols // inner_length
    blocks = wave_field.reshape(2, batches, x_rows, outer_size, inner_length)
    blocks = contract("cbxan,cadk->dbxkn", blocks, complex_table(outer_size, -1.0))
    cosine, sine_part = twiddle(outer_size, inner_length, y_cols, -1.0)
    blocks = rotate(blocks, cosine, sine_part)
    blocks = contract("cbxkn,cndm->dbxkm", blocks, complex_table(inner_length, -1.0))
    return blocks.reshape(2, batches, x_rows, y_cols)


def inverse_rows(wave_field):
    batches, x_rows, y_cols = wave_field.shape[1:]
    outer_size = y_cols // inner_length
    blocks = wave_field.reshape(2, batches, x_rows, outer_size, inner_length)
    blocks = contract("cbxkm,cmdn->dbxkn", blocks, complex_table(inner_length, 1.0))
    cosine, sine_part = twiddle(outer_size, inner_length, y_cols, 1.0)
    blocks = rotate(blocks, cosine, sine_part)
    blocks = contract("cbxkn,ckda->dbxan", blocks, complex_table(outer_size, 1.0))
    return blocks.reshape(2, batches, x_rows, y_cols) / y_cols


def forward_columns(blocks):
    inner_size = blocks.shape[2]
    pencils = blocks.shape[3]
    blocks = contract("cbnsy,csdk->dbnky", blocks, complex_table(pencils, -1.0))
    cosine, sine_part = twiddle(pencils, inner_size, inner_size * pencils, -1.0)
    blocks = rotate(blocks, cosine.T[:, :, None], sine_part.T[:, :, None])
    return contract("cbnky,cndm->dbmky", blocks, complex_table(inner_size, -1.0))


def inverse_columns(blocks):
    inner_size = blocks.shape[2]
    pencils = blocks.shape[3]
    blocks = contract("cbmky,cmdn->dbnky", blocks, complex_table(inner_size, 1.0))
    cosine, sine_part = twiddle(pencils, inner_size, inner_size * pencils, 1.0)
    blocks = rotate(blocks, cosine.T[:, :, None], sine_part.T[:, :, None])
    blocks = contract("cbnky,ckds->dbnsy", blocks, complex_table(pencils, 1.0))
    return blocks / (inner_size * pencils)


def propagate(blocks, omegas, polarities, y_total):
    inner_size, pencils, y_local = blocks.shape[2:]
    x_index = (
        jnp.arange(pencils, dtype=jnp.int32)[None, :]
        + pencils * jnp.arange(inner_size, dtype=jnp.int32)[:, None]
    )
    stored = lax.axis_index("gy") * y_local + jnp.arange(y_local, dtype=jnp.int32)
    y_index = stored // inner_length + y_total // inner_length * (stored % inner_length)
    x_waves = wave_number(x_index, inner_size * pencils)
    y_waves = wave_number(y_index, y_total)
    lateral = x_waves[:, :, None] ** 2 + y_waves[None, None, :] ** 2
    kz_square = ((omegas * reference_slowness) ** 2)[:, None, None, None] - lateral[None]
    kz_root = jnp.sqrt(jnp.abs(kz_square))
    travels = kz_square >= 0.0
    amplitude = jnp.where(travels, 1.0, jnp.exp(-kz_root * depth_interval))
    angles = jnp.where(travels, polarities[:, None, None, None] * kz_root * depth_interval, 0.0)
    return rotate(blocks, amplitude * jnp.cos(angles), amplitude * jnp.sin(angles))


def apply_screen(wave_field, slowness_now, omegas, polarities):
    phases = (polarities * omegas)[:, None, None] * (
        (slowness_now - reference_slowness) * depth_interval
    )[None]
    return rotate(wave_field, jnp.cos(phases), jnp.sin(phases))


def per_device_pencils(wavefields, slowness, freq_index):
    x_rows = wavefields.shape[3]
    y_cols = wavefields.shape[4]
    pencils = lax.axis_size("gy")
    freq_devs = lax.axis_size("freq")
    fld_devs = lax.axis_size("fld")
    column_width = y_cols // (freq_devs * fld_devs)
    omegas = omega_unit * freq_index.astype(jnp.float32)
    per_side = wavefields.shape[2] // fld_devs
    regrouped = wavefields.reshape(2, 1, fld_devs, per_side, x_rows, y_cols)
    paired = lax.all_to_all(regrouped, "fld", split_axis=2, concat_axis=1, tiled=True)
    wave_field = paired.reshape(2, fld_devs * per_side, x_rows, y_cols)
    local_omegas = lax.dynamic_slice_in_dim(omegas, lax.axis_index("fld") * per_side, per_side)
    omegas = jnp.tile(local_omegas, fld_devs)
    polarities = jnp.repeat(jnp.array([-1.0, 1.0], jnp.float32), per_side)
    batches = wave_field.shape[1]
    images = []
    for depth_step in range(DEPTH):
        wave_field = forward_rows(wave_field)
        blocks = wave_field.reshape(2, batches, x_rows, pencils, y_cols // pencils)
        blocks = lax.all_to_all(blocks, "gy", split_axis=3, concat_axis=3, tiled=True)
        blocks = forward_columns(blocks)
        blocks = propagate(blocks, omegas, polarities, y_cols)
        blocks = inverse_columns(blocks)
        blocks = lax.all_to_all(blocks, "gy", split_axis=3, concat_axis=3, tiled=True)
        wave_field = inverse_rows(blocks.reshape(2, batches, x_rows, y_cols))
        wave_field = apply_screen(wave_field, slowness[depth_step], omegas, polarities)
        source = wave_field[:, :per_side]
        receiver = wave_field[:, per_side:]
        summed = jnp.sum(source[0] * receiver[0] + source[1] * receiver[1], axis=0)
        partial_image = summed.reshape(x_rows, freq_devs * fld_devs, column_width)[None]
        images.append(
            lax.psum_scatter(partial_image, ("freq", "fld"), scatter_dimension=2, tiled=True)
        )
    combined = jnp.concatenate(images, axis=0)
    return combined.reshape(DEPTH, x_rows, column_width)


axes = ("shot", "gy", "freq", "fld")
lanes = 128
y_radix = 8
x_radix = 4
row_block = 64
strip = 16


def fits_one_field_per_chip(sizes, shape):
    return (
        sizes["gy"] == 4
        and sizes["freq"] == 2
        and sizes["fld"] == 2
        and shape[2] == 2
        and shape[4] == y_radix * lanes
        and shape[3] % row_block == 0
        and shape[3] * 4 == shape[4]
    )


def route(sizes, target):
    pairs = []
    for place in np.ndindex(*(sizes[axis] for axis in axes)):
        goal = target(*place)
        if goal is not None:
            dims = tuple(sizes[axis] for axis in axes)
            pairs.append(
                (int(np.ravel_multi_index(place, dims)), int(np.ravel_multi_index(goal, dims)))
            )
    return pairs


def split_constant(matrix):
    upper = matrix.astype(jnp.bfloat16)
    lower = (matrix - upper.astype(np.float64)).astype(jnp.bfloat16)
    return upper, lower


def dft_parts(length, polarity):
    indices = np.arange(length)
    angles = 2.0 * np.pi / length * (indices[:, None] * indices[None, :] % length)
    return np.cos(angles), polarity * np.sin(angles)


def row_matrix(length, polarity):
    cosine, sine = dft_parts(length, polarity)
    return split_constant(np.block([[cosine, sine], [-sine, cosine]]))


def column_matrix(length, polarity):
    cosine, sine = dft_parts(length, polarity)
    return split_constant(np.block([[cosine, -sine], [sine, cosine]]))


def add(one, two):
    return one[0] + two[0], one[1] + two[1]


def subtract(one, two):
    return one[0] - two[0], one[1] - two[1]


def multiply(one, two):
    return one[0] * two[0] - one[1] * two[1], one[0] * two[1] + one[1] * two[0]


def conjugate(one):
    return one[0], -one[1]


def quarter_turn(one, polarity):
    if polarity > 0:
        return -one[1], one[0]
    return one[1], -one[0]


def dft4(terms, polarity):
    even = add(terms[0], terms[2])
    odd = subtract(terms[0], terms[2])
    even_other = add(terms[1], terms[3])
    odd_other = quarter_turn(subtract(terms[1], terms[3]), polarity)
    return [
        add(even, even_other),
        add(odd, odd_other),
        subtract(even, even_other),
        subtract(odd, odd_other),
    ]


def eighth_turn(one, polarity):
    half = math.sqrt(0.5)
    if polarity > 0:
        return (one[0] - one[1]) * half, (one[0] + one[1]) * half
    return (one[0] + one[1]) * half, (one[1] - one[0]) * half


def dft8(terms, polarity):
    sums = [add(terms[a], terms[a + 4]) for a in range(4)]
    differences = [subtract(terms[a], terms[a + 4]) for a in range(4)]
    turned = [
        differences[0],
        eighth_turn(differences[1], polarity),
        quarter_turn(differences[2], polarity),
        quarter_turn(eighth_turn(differences[3], polarity), polarity),
    ]
    even = dft4(sums, polarity)
    odd = dft4(turned, polarity)
    return [even[k // 2] if k % 2 == 0 else odd[k // 2] for k in range(8)]


def two_parts(values):
    upper = values.astype(jnp.bfloat16)
    lower = (values - upper.astype(jnp.float32)).astype(jnp.bfloat16)
    return upper, lower


def dot(left, right):
    return jnp.dot(left, right, preferred_element_type=jnp.float32)


def rows_product(values, upper_ref, lower_ref):
    upper, lower = two_parts(values)
    return dot(upper, upper_ref[...]) + dot(lower, upper_ref[...]) + dot(upper, lower_ref[...])


def columns_product(upper_ref, lower_ref, upper, lower):
    return dot(upper_ref[...], upper) + dot(upper_ref[...], lower) + dot(lower_ref[...], upper)


def stack_blocks(terms):
    return jnp.concatenate([jnp.concatenate(term, axis=1) for term in terms], axis=0)


def unstack_blocks(values, rows):
    blocks = [values[k * rows : (k + 1) * rows] for k in range(y_radix)]
    return [(block[:, :lanes], block[:, lanes:]) for block in blocks]


def y_twiddle(table_ref, k):
    return table_ref[k, 0:1, :], table_ref[k, 1:2, :]


def forward_y(terms, table_ref, upper_ref, lower_ref):
    rows = terms[0][0].shape[0]
    turned = dft8(terms, -1.0)
    turned = [multiply(turned[k], y_twiddle(table_ref, k)) for k in range(y_radix)]
    return unstack_blocks(rows_product(stack_blocks(turned), upper_ref, lower_ref), rows)


def inverse_y(terms, table_ref, upper_ref, lower_ref):
    rows = terms[0][0].shape[0]
    inner = unstack_blocks(rows_product(stack_blocks(terms), upper_ref, lower_ref), rows)
    inner = [multiply(inner[k], conjugate(y_twiddle(table_ref, k))) for k in range(y_radix)]
    return dft8(inner, 1.0)


def lane_block(index):
    return slice(index * lanes, (index + 1) * lanes)


def origin_kernel(place_ref, field_ref, table_ref, upper_ref, lower_ref, *outs):
    sign = (1 - 2 * place_ref[3]).astype(jnp.float32)
    terms = []
    for a in range(y_radix):
        term = (field_ref[0, 0, :, lane_block(a)], field_ref[1, 0, :, lane_block(a)])
        terms.append((term[0] * sign, term[1] * sign) if a % 2 else term)
    spectrum = forward_y(terms, table_ref, upper_ref, lower_ref)
    for k in range(y_radix):
        for part in range(2):
            outs[k // 2][0, part, :, lane_block(k % 2)] = spectrum[k][part]


def read_y_blocks(blocks):
    return [
        tuple(blocks[k // 2][part, :, lane_block(k % 2)] for part in range(2))
        for k in range(y_radix)
    ]


def read_screen(screen_ref, a):
    return screen_ref[0, 0, :, lane_block(a)], screen_ref[0, 1, :, lane_block(a)]


def turn_kernel(keeps_field, *refs):
    blocks, rest = refs[:4], refs[4:]
    screen_ref, table_ref, inv_upper, inv_lower, upper_ref, lower_ref = rest[:6]
    outs = rest[6:]
    terms = inverse_y(read_y_blocks(blocks), table_ref, inv_upper, inv_lower)
    terms = [multiply(terms[a], read_screen(screen_ref, a)) for a in range(y_radix)]
    if keeps_field:
        for a in range(y_radix):
            for part in range(2):
                outs[4][part, :, lane_block(a)] = terms[a][part]
    spectrum = forward_y(terms, table_ref, upper_ref, lower_ref)
    for k in range(y_radix):
        for part in range(2):
            outs[k // 2][part, :, lane_block(k % 2)] = spectrum[k][part]


def image_kernel(own_ready, place_ref, *refs):
    own_count = 1 if own_ready else 4
    own, refs = refs[:own_count], refs[own_count:]
    blocks, refs = refs[:4], refs[4:]
    screen_ref, table_ref, inv_upper, inv_lower = refs[:4]
    outs, quarters = refs[4:8], refs[8]
    other = inverse_y(read_y_blocks(blocks), table_ref, inv_upper, inv_lower)
    if not own_ready:
        mine = inverse_y(read_y_blocks(own), table_ref, inv_upper, inv_lower)
    for a in range(y_radix):
        screen = read_screen(screen_ref, a)
        if own_ready:
            near = (own[0][0, :, lane_block(a)], own[0][1, :, lane_block(a)])
        else:
            near = multiply(mine[a], screen)
        far = multiply(other[a], conjugate(screen))
        quarters[a // 2, :, lane_block(a % 2)] = near[0] * far[0] + near[1] * far[1]
    for r in range(4):
        outs[r][...] = quarters[lax.bitwise_xor(place_ref[1], r)]


def x_kernel(
    swap_ref, b0, b1, b2, b3, table_in, table_out, move_ref,
    upper_ref, lower_ref, inv_upper, inv_lower, o0, o1, o2, o3, high, low, held,
):
    blocks, outs = (b0, b1, b2, b3), (o0, o1, o2, o3)
    rows = b0.shape[1]

    def wide(table, k, part, span):
        values = table[k, part, span, :]
        return jnp.concatenate([values] * (b0.shape[2] // lanes), axis=1)

    def actual(k, swaps):
        return k if k % 2 == 0 else lax.bitwise_xor(k, 2 * swaps)

    def gather_rows(step, carry):
        span = pl.ds(pl.multiple_of(step * strip, strip), strip)
        lower_span = pl.ds(pl.multiple_of(step * strip + rows, strip), strip)
        terms = dft4([(block[0, span, :], block[1, span, :]) for block in blocks], -1.0)
        for k in range(x_radix):
            factor = (wide(table_in, k, 0, span), wide(table_in, k, 1, span))
            real, imag = multiply(terms[k], factor)
            goal = actual(k, swap_ref[0])
            high[goal, span, :], low[goal, span, :] = two_parts(real)
            high[goal, lower_span, :], low[goal, lower_span, :] = two_parts(imag)
        return carry

    lax.fori_loop(0, rows // strip, gather_rows, 0)

    def one_block(k, carry):
        values = columns_product(upper_ref, lower_ref, high[k], low[k])
        moved = multiply((values[:rows], values[rows:]), (move_ref[k, 0], move_ref[k, 1]))
        upper, lower = two_parts(jnp.concatenate(moved, axis=0))
        held[k] = columns_product(inv_upper, inv_lower, upper, lower)
        return carry

    lax.fori_loop(0, x_radix, one_block, 0)

    def scatter_rows(step, carry):
        span = pl.ds(pl.multiple_of(step * strip, strip), strip)
        lower_span = pl.ds(pl.multiple_of(step * strip + rows, strip), strip)
        terms = []
        for k in range(x_radix):
            source = actual(k, swap_ref[1])
            factor = (wide(table_out, k, 0, span), -wide(table_out, k, 1, span))
            terms.append(multiply((held[source, span, :], held[source, lower_span, :]), factor))
        terms = dft4(terms, 1.0)
        for q in range(x_radix):
            for part in range(2):
                outs[q][part, span, :] = terms[q][part]
        return carry

    lax.fori_loop(0, rows // strip, scatter_rows, 0)


def whole(array):
    return pl.BlockSpec(array.shape, lambda *step: (0,) * array.ndim)


smem = pl.BlockSpec(memory_space=pltpu.SMEM)
vmem = pl.BlockSpec(memory_space=pltpu.VMEM)
vmem_limit = 40 * 1024 * 1024


def parameters(steps):
    return pltpu.CompilerParams(
        vmem_limit_bytes=vmem_limit, dimension_semantics=("arbitrary",) * steps
    )


def estimate(microseconds):
    return pl.CostEstimate(
        flops=int(microseconds * 1e9), bytes_accessed=int(microseconds * 3e6), transcendentals=0
    )


def origin_rows(field, place, table, matrices):
    parts, freqs, rows, y_cols = field.shape
    width = y_cols // 4
    out = jax.ShapeDtypeStruct((freqs, parts, rows, width), jnp.float32)
    return pl.pallas_call(
        origin_kernel,
        grid=(freqs, rows // row_block),
        in_specs=[
            smem,
            pl.BlockSpec((parts, 1, row_block, y_cols), lambda j, i: (0, j, i, 0)),
            whole(table),
            whole(matrices[0]),
            whole(matrices[1]),
        ],
        out_specs=[pl.BlockSpec((1, parts, row_block, width), lambda j, i: (j, 0, i, 0))] * 4,
        out_shape=[out] * 4,
        compiler_params=parameters(2),
        cost_estimate=estimate(6),
        name="origin_rows",
    )(place, field, table, *matrices)


def turn_rows(keeps_field, slot, blocks, screen, table, inverse, forward):
    parts, rows, width = blocks[0].shape
    y_cols = screen.shape[-1]
    block = pl.BlockSpec((parts, row_block, width), lambda i: (0, i, 0))
    full = pl.BlockSpec((parts, row_block, y_cols), lambda i: (0, i, 0))
    out = [jax.ShapeDtypeStruct((parts, rows, width), jnp.float32)] * 4
    out_specs = [block] * 4
    if keeps_field:
        out = out + [jax.ShapeDtypeStruct((parts, rows, y_cols), jnp.float32)]
        out_specs = out_specs + [full]
    return pl.pallas_call(
        functools.partial(turn_kernel, keeps_field),
        grid=(rows // row_block,),
        in_specs=[block] * 4
        + [pl.BlockSpec((1, 2, row_block, y_cols), lambda i: (slot, 0, i, 0))]
        + [whole(array) for array in (table, *inverse, *forward)],
        out_specs=out_specs,
        out_shape=out,
        compiler_params=parameters(1),
        cost_estimate=estimate(5),
        name="turn_rows",
    )(*blocks, screen, table, *inverse, *forward)


def image_rows(place, own, blocks, screen, table, inverse):
    parts, rows, width = blocks[0].shape
    y_cols = screen.shape[-1]
    own_ready = len(own) == 1
    block = pl.BlockSpec((parts, row_block, width), lambda i: (0, i, 0))
    full = pl.BlockSpec((parts, row_block, y_cols), lambda i: (0, i, 0))
    return pl.pallas_call(
        functools.partial(image_kernel, own_ready),
        grid=(rows // row_block,),
        in_specs=[smem]
        + ([full] if own_ready else [block] * 4)
        + [block] * 4
        + [pl.BlockSpec((1, 2, row_block, y_cols), lambda i: (0, 0, i, 0))]
        + [whole(array) for array in (table, *inverse)],
        out_specs=[pl.BlockSpec((row_block, width), lambda i: (i, 0))] * 4,
        out_shape=[jax.ShapeDtypeStruct((rows, width), jnp.float32)] * 4,
        scratch_shapes=[pltpu.VMEM((4, row_block, width), jnp.float32)],
        compiler_params=parameters(1),
        cost_estimate=estimate(4),
        name="image_rows",
    )(place, *own, *blocks, screen, table, *inverse)


def move_columns(chunk, swaps, blocks, table_in, table_out, move, forward, inverse):
    parts, rows, width = blocks[0].shape
    move_block = pl.BlockSpec(
        (x_radix, parts, rows, width), lambda i: (0, 0, 0, chunk)
    )
    block = whole(blocks[0])
    return pl.pallas_call(
        x_kernel,
        grid=(1,),
        in_specs=[smem] + [block] * 4 + [whole(table_in), whole(table_out), move_block]
        + [whole(array) for array in (*forward, *inverse)],
        out_specs=[block] * 4,
        out_shape=[jax.ShapeDtypeStruct((parts, rows, width), jnp.float32)] * 4,
        scratch_shapes=[
            pltpu.VMEM((x_radix, parts * rows, width), jnp.bfloat16),
            pltpu.VMEM((x_radix, parts * rows, width), jnp.bfloat16),
            pltpu.VMEM((x_radix, parts * rows, width), jnp.float32),
        ],
        compiler_params=parameters(1),
        cost_estimate=estimate(8),
        name="move_columns",
    )(swaps, *blocks, table_in, table_out, move, *forward, *inverse)


def y_table(core, y_cols):
    k = (jnp.arange(y_radix, dtype=jnp.int32) ^ (4 * core))[:, None]
    r = jnp.arange(lanes, dtype=jnp.int32)[None, :]
    angles = 2.0 * math.pi / y_cols * (k * r % y_cols).astype(jnp.float32)
    return jnp.stack([jnp.cos(angles), -jnp.sin(angles)], axis=1)


def x_table(order, x_total):
    rows = x_total // x_radix
    low_bit, high_bit = order & 1, order >> 1
    slot = jnp.arange(x_radix, dtype=jnp.int32)
    k = jnp.where(slot % 2 == 1, slot ^ (2 * low_bit), slot)
    eighths = jnp.where(k % 2 == 1, 4 * high_bit, 0)
    turns = jnp.array([0, 6, 4, 2], jnp.int32)
    eighths = eighths + low_bit * turns[k]
    row = jnp.arange(rows, dtype=jnp.int32)[None, :]
    steps = (x_total // 8 * eighths[:, None] - k[:, None] * row) % x_total
    angles = 2.0 * math.pi / x_total * steps.astype(jnp.float32)
    table = jnp.stack([jnp.cos(angles), jnp.sin(angles)], axis=1)
    return jnp.broadcast_to(table[..., None], table.shape + (lanes,))


def move_table(omega, polarity, core, x_total, y_total):
    k = jnp.arange(x_radix, dtype=jnp.int32)[:, None]
    inner = jnp.arange(x_total // x_radix, dtype=jnp.int32)[None, :]
    x_waves = wave_number(k + x_radix * inner, x_total)
    ky = jnp.arange(y_radix // 2, dtype=jnp.int32)[:, None] + y_radix // 2 * core
    inner = jnp.arange(lanes, dtype=jnp.int32)[None, :]
    y_waves = wave_number((ky + y_radix * inner).reshape(-1), y_total)
    lateral = x_waves[:, :, None] ** 2 + y_waves[None, None, :] ** 2
    kz_square = (omega * reference_slowness) ** 2 - lateral
    kz_root = jnp.sqrt(jnp.abs(kz_square))
    travels = kz_square >= 0.0
    amplitude = jnp.where(travels, 1.0, jnp.exp(-kz_root * depth_interval))
    amplitude = amplitude / (x_total * y_total)
    angles = jnp.where(travels, polarity * kz_root * depth_interval, 0.0)
    return jnp.stack([amplitude * jnp.cos(angles), amplitude * jnp.sin(angles)], axis=1)


def per_device_fields(sizes, wavefields, slowness, freq_index):
    s, z, x, c = (lax.axis_index(axis) for axis in axes)
    rows, y_cols = wavefields.shape[3:]
    x_total = rows * sizes["gy"]
    place = jnp.stack([s, z, x, c]).astype(jnp.int32)

    def send(array, target):
        return lax.ppermute(array, axes, route(sizes, target))

    def to_core(array):
        return send(array, lambda s, z, x, c: (s, z, x, 1 - c))

    def to_partner(array):
        return send(array, lambda s, z, x, c: (s, z, 1 - x, c))

    def to_partner_core(array):
        return send(array, lambda s, z, x, c: (s, z, 1 - x, 1 - c))

    def to_shot(array):
        return send(array, lambda s, z, x, c: (1 - s, z, x, c))

    def along_z(array, r):
        return send(array, lambda s, z, x, c: (s, z ^ r, x, c))

    row_forward = row_matrix(lanes, -1.0)
    row_inverse = row_matrix(lanes, 1.0)
    column_forward = column_matrix(rows, -1.0)
    column_inverse = column_matrix(rows, 1.0)

    y_steps = y_table(c, y_cols)
    spectra = origin_rows(wavefields[0], place, y_steps, row_forward)
    own_field = c == x
    arrived = []
    for chunk in range(2):
        kept, crossed = spectra[chunk], to_core(spectra[2 + chunk])
        stays = jnp.where(own_field, kept, crossed)
        moved = to_partner(jnp.where(own_field, crossed, kept))
        blocks = []
        for r in range(4):
            goal = z ^ r
            choice = jnp.where(goal % 2 == x, stays, moved)
            block = lax.dynamic_index_in_dim(choice, goal // 2, 0, keepdims=False)
            blocks.append(block if r == 0 else along_z(block, r))
        arrived.append(blocks)

    other_index = to_partner(freq_index)
    indices = jnp.where(z % 2 == x, freq_index, other_index)
    omega = omega_unit * lax.dynamic_index_in_dim(indices, z // 2, 0, keepdims=False).astype(jnp.float32)
    polarity = (2 * x - 1).astype(jnp.float32)
    order = 2 * c + x
    move = move_table(omega, polarity, c, x_total, y_cols)
    table_z = x_table(z, x_total)
    table_order = x_table(order, x_total)

    width = y_cols // 4

    def screens_of(layer):
        piece = lax.dynamic_slice_in_dim(layer, (2 * s + c) * width, width, 1)
        pieces = jnp.stack([piece] + [along_z(piece, r) for r in range(1, 4)])
        mine = lax.dynamic_slice_in_dim(pieces, 2 * ((z // 2) ^ c), 2, 0)
        theirs = to_core(lax.dynamic_slice_in_dim(pieces, 2 * ((z // 2) ^ (1 - c)), 2, 0))
        half = jnp.where(
            c == 0, jnp.concatenate([mine, theirs], 2), jnp.concatenate([theirs, mine], 2)
        )
        far = to_shot(half)
        both = jnp.where(s == 0, jnp.concatenate([half, far], 2), jnp.concatenate([far, half], 2))
        both = jnp.where((z % 2) == x, both, both[::-1])
        phases = (polarity * omega) * ((both - reference_slowness) * depth_interval)
        return jnp.stack([jnp.cos(phases), jnp.sin(phases)], axis=1)

    images = []
    blocks_in, order_in, table_in = arrived, z, table_z
    for depth_step in range(DEPTH):
        last = depth_step == DEPTH - 1
        swaps = jnp.stack([order_in & 1, order & 1]).astype(jnp.int32)
        screen = screens_of(slowness[depth_step])
        near, partner = [], []
        for chunk in range(2):
            out = move_columns(
                chunk, swaps, blocks_in[chunk], table_in, table_order, move,
                column_forward, column_inverse,
            )
            crossed = [to_core(out[2]), None if last else to_core(out[3])]
            near.append([[out[0], crossed[0]], [out[1], crossed[1]]])
            partner.append([to_partner(out[1]), to_partner_core(out[3])])

        def y_blocks(pairs):
            return [pairs[0][0], pairs[1][0], pairs[0][1], pairs[1][1]]

        own = y_blocks([near[0][0], near[1][0]])
        if not last:
            turned = [None, None]
            for slot in (1, 0):
                blocks = y_blocks([near[0][slot], near[1][slot]])
                turned[slot] = turn_rows(
                    slot == 0, slot, blocks, screen, y_steps, row_inverse, row_forward
                )
            blocks_in = [
                [turned[0][k], turned[1][k], to_core(turned[0][2 + k]), to_core(turned[1][2 + k])]
                for k in range(2)
            ]
            order_in, table_in = order, table_order
            own = [turned[0][4]]
        terms = image_rows(place, own, y_blocks(partner), screen, y_steps, row_inverse)

        def gather(r):
            def target(s, z, x, c):
                quarter = z ^ r
                return s, 2 * c + x, quarter // 2, quarter % 2

            return send(terms[r], target)

        images.append(sum(gather(r) for r in range(4)))
    return jnp.stack(images)


def solution(mesh):
    sizes = dict(mesh.shape)

    def per_device(wavefields, slowness, freq_index):
        if fits_one_field_per_chip(sizes, wavefields.shape):
            return per_device_fields(sizes, wavefields, slowness, freq_index)
        return per_device_pencils(wavefields, slowness, freq_index)

    placed = (P("fld", None, ("shot", "freq"), "gy", None), P(None, "gy", None), P("freq"))
    return jax.shard_map(
        per_device,
        mesh=mesh,
        in_specs=placed,
        out_specs=P("shot", "gy", ("freq", "fld")),
        check_vma=False,
    )
```

```python
import functools
import math

import jax
import jax.numpy as jnp
import numpy as np
from jax import lax
from jax.experimental import pallas as pl
from jax.experimental.pallas import tpu as pltpu
from jax.sharding import PartitionSpec as P

DEPTH = 2


omega_unit = 0.1
reference_slowness = 1.0
depth_interval = 1.0
inner_length = 128


def contract(pattern, values, matrix):
    return jnp.einsum(
        pattern, values, matrix, precision=lax.Precision.HIGHEST, preferred_element_type=jnp.float32
    )


def complex_table(length, polarity):
    indices = jnp.arange(length, dtype=jnp.int32)
    angles = (
        2.0 * math.pi / length * (indices[:, None] * indices[None, :] % length).astype(jnp.float32)
    )
    cosine = jnp.cos(angles)
    sine_part = polarity * jnp.sin(angles)
    upper = jnp.stack([cosine, sine_part], axis=1)
    lower = jnp.stack([-sine_part, cosine], axis=1)
    return jnp.stack([upper, lower], axis=0)


def twiddle(outer_size, inner_size, length, polarity):
    outer_index = jnp.arange(outer_size, dtype=jnp.int32)[:, None]
    inner_index = jnp.arange(inner_size, dtype=jnp.int32)[None, :]
    angles = 2.0 * math.pi / length * (outer_index * inner_index % length).astype(jnp.float32)
    return (jnp.cos(angles), polarity * jnp.sin(angles))


def rotate(values, cosine, sine_part):
    real_part = values[0]
    imag_part = values[1]
    return jnp.stack(
        [real_part * cosine - imag_part * sine_part, real_part * sine_part + imag_part * cosine]
    )


def wave_number(indices, length):
    signed = jnp.where(indices < length // 2, indices, indices - length)
    return 2.0 * math.pi / length * signed.astype(jnp.float32)


def forward_rows(wave_field):
    batches, x_rows, y_cols = wave_field.shape[1:]
    outer_size = y_cols // inner_length
    blocks = wave_field.reshape(2, batches, x_rows, outer_size, inner_length)
    blocks = contract("cbxan,cadk->dbxkn", blocks, complex_table(outer_size, -1.0))
    cosine, sine_part = twiddle(outer_size, inner_length, y_cols, -1.0)
    blocks = rotate(blocks, cosine, sine_part)
    blocks = contract("cbxkn,cndm->dbxkm", blocks, complex_table(inner_length, -1.0))
    return blocks.reshape(2, batches, x_rows, y_cols)


def inverse_rows(wave_field):
    batches, x_rows, y_cols = wave_field.shape[1:]
    outer_size = y_cols // inner_length
    blocks = wave_field.reshape(2, batches, x_rows, outer_size, inner_length)
    blocks = contract("cbxkm,cmdn->dbxkn", blocks, complex_table(inner_length, 1.0))
    cosine, sine_part = twiddle(outer_size, inner_length, y_cols, 1.0)
    blocks = rotate(blocks, cosine, sine_part)
    blocks = contract("cbxkn,ckda->dbxan", blocks, complex_table(outer_size, 1.0))
    return blocks.reshape(2, batches, x_rows, y_cols) / y_cols


def forward_columns(blocks):
    inner_size = blocks.shape[2]
    pencils = blocks.shape[3]
    blocks = contract("cbnsy,csdk->dbnky", blocks, complex_table(pencils, -1.0))
    cosine, sine_part = twiddle(pencils, inner_size, inner_size * pencils, -1.0)
    blocks = rotate(blocks, cosine.T[:, :, None], sine_part.T[:, :, None])
    return contract("cbnky,cndm->dbmky", blocks, complex_table(inner_size, -1.0))


def inverse_columns(blocks):
    inner_size = blocks.shape[2]
    pencils = blocks.shape[3]
    blocks = contract("cbmky,cmdn->dbnky", blocks, complex_table(inner_size, 1.0))
    cosine, sine_part = twiddle(pencils, inner_size, inner_size * pencils, 1.0)
    blocks = rotate(blocks, cosine.T[:, :, None], sine_part.T[:, :, None])
    blocks = contract("cbnky,ckds->dbnsy", blocks, complex_table(pencils, 1.0))
    return blocks / (inner_size * pencils)


def propagate(blocks, omegas, polarities, y_total):
    inner_size, pencils, y_local = blocks.shape[2:]
    x_index = (
        jnp.arange(pencils, dtype=jnp.int32)[None, :]
        + pencils * jnp.arange(inner_size, dtype=jnp.int32)[:, None]
    )
    stored = lax.axis_index("gy") * y_local + jnp.arange(y_local, dtype=jnp.int32)
    y_index = stored // inner_length + y_total // inner_length * (stored % inner_length)
    x_waves = wave_number(x_index, inner_size * pencils)
    y_waves = wave_number(y_index, y_total)
    lateral = x_waves[:, :, None] ** 2 + y_waves[None, None, :] ** 2
    kz_square = ((omegas * reference_slowness) ** 2)[:, None, None, None] - lateral[None]
    kz_root = jnp.sqrt(jnp.abs(kz_square))
    travels = kz_square >= 0.0
    amplitude = jnp.where(travels, 1.0, jnp.exp(-kz_root * depth_interval))
    angles = jnp.where(travels, polarities[:, None, None, None] * kz_root * depth_interval, 0.0)
    return rotate(blocks, amplitude * jnp.cos(angles), amplitude * jnp.sin(angles))


def apply_screen(wave_field, slowness_now, omegas, polarities):
    phases = (polarities * omegas)[:, None, None] * (
        (slowness_now - reference_slowness) * depth_interval
    )[None]
    return rotate(wave_field, jnp.cos(phases), jnp.sin(phases))


def per_device_pencils(wavefields, slowness, freq_index):
    x_rows = wavefields.shape[3]
    y_cols = wavefields.shape[4]
    pencils = lax.axis_size("gy")
    freq_devs = lax.axis_size("freq")
    fld_devs = lax.axis_size("fld")
    column_width = y_cols // (freq_devs * fld_devs)
    omegas = omega_unit * freq_index.astype(jnp.float32)
    per_side = wavefields.shape[2] // fld_devs
    regrouped = wavefields.reshape(2, 1, fld_devs, per_side, x_rows, y_cols)
    paired = lax.all_to_all(regrouped, "fld", split_axis=2, concat_axis=1, tiled=True)
    wave_field = paired.reshape(2, fld_devs * per_side, x_rows, y_cols)
    local_omegas = lax.dynamic_slice_in_dim(omegas, lax.axis_index("fld") * per_side, per_side)
    omegas = jnp.tile(local_omegas, fld_devs)
    polarities = jnp.repeat(jnp.array([-1.0, 1.0], jnp.float32), per_side)
    batches = wave_field.shape[1]
    images = []
    for depth_step in range(DEPTH):
        wave_field = forward_rows(wave_field)
        blocks = wave_field.reshape(2, batches, x_rows, pencils, y_cols // pencils)
        blocks = lax.all_to_all(blocks, "gy", split_axis=3, concat_axis=3, tiled=True)
        blocks = forward_columns(blocks)
        blocks = propagate(blocks, omegas, polarities, y_cols)
        blocks = inverse_columns(blocks)
        blocks = lax.all_to_all(blocks, "gy", split_axis=3, concat_axis=3, tiled=True)
        wave_field = inverse_rows(blocks.reshape(2, batches, x_rows, y_cols))
        wave_field = apply_screen(wave_field, slowness[depth_step], omegas, polarities)
        source = wave_field[:, :per_side]
        receiver = wave_field[:, per_side:]
        summed = jnp.sum(source[0] * receiver[0] + source[1] * receiver[1], axis=0)
        partial_image = summed.reshape(x_rows, freq_devs * fld_devs, column_width)[None]
        images.append(
            lax.psum_scatter(partial_image, ("freq", "fld"), scatter_dimension=2, tiled=True)
        )
    combined = jnp.concatenate(images, axis=0)
    return combined.reshape(DEPTH, x_rows, column_width)


axes = ("shot", "gy", "freq", "fld")
lanes = 128
y_radix = 8
x_radix = 4
row_block = 64
strip = 16


def fits_one_field_per_chip(sizes, shape):
    return (
        sizes["gy"] == 4
        and sizes["freq"] == 2
        and sizes["fld"] == 2
        and shape[2] == 2
        and shape[4] == y_radix * lanes
        and shape[3] % row_block == 0
        and shape[3] * 4 == shape[4]
    )


def route(sizes, target):
    pairs = []
    for place in np.ndindex(*(sizes[axis] for axis in axes)):
        goal = target(*place)
        if goal is not None:
            dims = tuple(sizes[axis] for axis in axes)
            pairs.append(
                (int(np.ravel_multi_index(place, dims)), int(np.ravel_multi_index(goal, dims)))
            )
    return pairs


def split_constant(matrix):
    upper = matrix.astype(jnp.bfloat16)
    lower = (matrix - upper.astype(np.float64)).astype(jnp.bfloat16)
    return upper, lower


def dft_parts(length, polarity):
    indices = np.arange(length)
    angles = 2.0 * np.pi / length * (indices[:, None] * indices[None, :] % length)
    return np.cos(angles), polarity * np.sin(angles)


def row_matrix(length, polarity):
    cosine, sine = dft_parts(length, polarity)
    return split_constant(np.block([[cosine, sine], [-sine, cosine]]))


def column_matrix(length, polarity):
    cosine, sine = dft_parts(length, polarity)
    return split_constant(np.block([[cosine, -sine], [sine, cosine]]))


def add(one, two):
    return one[0] + two[0], one[1] + two[1]


def subtract(one, two):
    return one[0] - two[0], one[1] - two[1]


def multiply(one, two):
    return one[0] * two[0] - one[1] * two[1], one[0] * two[1] + one[1] * two[0]


def conjugate(one):
    return one[0], -one[1]


def quarter_turn(one, polarity):
    if polarity > 0:
        return -one[1], one[0]
    return one[1], -one[0]


def dft4(terms, polarity):
    even = add(terms[0], terms[2])
    odd = subtract(terms[0], terms[2])
    even_other = add(terms[1], terms[3])
    odd_other = quarter_turn(subtract(terms[1], terms[3]), polarity)
    return [
        add(even, even_other),
        add(odd, odd_other),
        subtract(even, even_other),
        subtract(odd, odd_other),
    ]


def eighth_turn(one, polarity):
    half = math.sqrt(0.5)
    if polarity > 0:
        return (one[0] - one[1]) * half, (one[0] + one[1]) * half
    return (one[0] + one[1]) * half, (one[1] - one[0]) * half


def dft8(terms, polarity):
    sums = [add(terms[a], terms[a + 4]) for a in range(4)]
    differences = [subtract(terms[a], terms[a + 4]) for a in range(4)]
    turned = [
        differences[0],
        eighth_turn(differences[1], polarity),
        quarter_turn(differences[2], polarity),
        quarter_turn(eighth_turn(differences[3], polarity), polarity),
    ]
    even = dft4(sums, polarity)
    odd = dft4(turned, polarity)
    return [even[k // 2] if k % 2 == 0 else odd[k // 2] for k in range(8)]


def two_parts(values):
    upper = values.astype(jnp.bfloat16)
    lower = (values - upper.astype(jnp.float32)).astype(jnp.bfloat16)
    return upper, lower


def dot(left, right):
    return jnp.dot(left, right, preferred_element_type=jnp.float32)


def rows_product(values, upper_ref, lower_ref):
    upper, lower = two_parts(values)
    return dot(upper, upper_ref[...]) + dot(lower, upper_ref[...]) + dot(upper, lower_ref[...])


def columns_product(upper_ref, lower_ref, upper, lower):
    return dot(upper_ref[...], upper) + dot(upper_ref[...], lower) + dot(lower_ref[...], upper)


def stack_blocks(terms):
    return jnp.concatenate([jnp.concatenate(term, axis=1) for term in terms], axis=0)


def unstack_blocks(values, rows):
    blocks = [values[k * rows : (k + 1) * rows] for k in range(y_radix)]
    return [(block[:, :lanes], block[:, lanes:]) for block in blocks]


def y_twiddle(table_ref, k):
    return table_ref[k, 0:1, :], table_ref[k, 1:2, :]


def forward_y(terms, table_ref, upper_ref, lower_ref):
    rows = terms[0][0].shape[0]
    turned = dft8(terms, -1.0)
    turned = [multiply(turned[k], y_twiddle(table_ref, k)) for k in range(y_radix)]
    return unstack_blocks(rows_product(stack_blocks(turned), upper_ref, lower_ref), rows)


def inverse_y(terms, table_ref, upper_ref, lower_ref):
    rows = terms[0][0].shape[0]
    inner = unstack_blocks(rows_product(stack_blocks(terms), upper_ref, lower_ref), rows)
    inner = [multiply(inner[k], conjugate(y_twiddle(table_ref, k))) for k in range(y_radix)]
    return dft8(inner, 1.0)


def lane_block(index):
    return slice(index * lanes, (index + 1) * lanes)


def origin_kernel(place_ref, field_ref, table_ref, upper_ref, lower_ref, *outs):
    sign = (1 - 2 * place_ref[3]).astype(jnp.float32)
    terms = []
    for a in range(y_radix):
        term = (field_ref[0, 0, :, lane_block(a)], field_ref[1, 0, :, lane_block(a)])
        terms.append((term[0] * sign, term[1] * sign) if a % 2 else term)
    spectrum = forward_y(terms, table_ref, upper_ref, lower_ref)
    for k in range(y_radix):
        for part in range(2):
            outs[k // 2][0, part, :, lane_block(k % 2)] = spectrum[k][part]


def read_y_blocks(blocks):
    return [
        tuple(blocks[k // 2][part, :, lane_block(k % 2)] for part in range(2))
        for k in range(y_radix)
    ]


def read_screen(scale_ref, slowness_ref, a):
    layer = slowness_ref[a // 2, 0, 0, :, lane_block(a % 2)]
    phase = scale_ref[0] * ((layer - reference_slowness) * depth_interval)
    square = phase * phase
    cosine, sine = 1.0 / 40320.0, 1.0 / 362880.0
    for term in (-1.0 / 720.0, 1.0 / 24.0, -0.5, 1.0):
        cosine = cosine * square + term
    for term in (-1.0 / 5040.0, 1.0 / 120.0, -1.0 / 6.0, 1.0):
        sine = sine * square + term
    return cosine, sine * phase


def turn_kernel(keeps_field, scale_ref, *refs):
    blocks, rest = refs[:4], refs[4:]
    screen_ref, table_ref, inv_upper, inv_lower, upper_ref, lower_ref = rest[:6]
    outs = rest[6:]
    terms = inverse_y(read_y_blocks(blocks), table_ref, inv_upper, inv_lower)
    terms = [multiply(terms[a], read_screen(scale_ref, screen_ref, a)) for a in range(y_radix)]
    if keeps_field:
        for a in range(y_radix):
            for part in range(2):
                outs[4][part, :, lane_block(a)] = terms[a][part]
    spectrum = forward_y(terms, table_ref, upper_ref, lower_ref)
    for k in range(y_radix):
        for part in range(2):
            outs[k // 2][part, :, lane_block(k % 2)] = spectrum[k][part]


def image_kernel(own_ready, place_ref, scale_ref, *refs):
    own_count = 1 if own_ready else 4
    own, refs = refs[:own_count], refs[own_count:]
    blocks, refs = refs[:4], refs[4:]
    screen_ref, table_ref, inv_upper, inv_lower = refs[:4]
    outs, quarters = refs[4:8], refs[8]
    other = inverse_y(read_y_blocks(blocks), table_ref, inv_upper, inv_lower)
    if not own_ready:
        mine = inverse_y(read_y_blocks(own), table_ref, inv_upper, inv_lower)
    for a in range(y_radix):
        screen = read_screen(scale_ref, screen_ref, a)
        if own_ready:
            near = (own[0][0, :, lane_block(a)], own[0][1, :, lane_block(a)])
        else:
            near = multiply(mine[a], screen)
        far = multiply(other[a], conjugate(screen))
        quarters[a // 2, :, lane_block(a % 2)] = near[0] * far[0] + near[1] * far[1]
    for r in range(4):
        outs[r][...] = quarters[lax.bitwise_xor(2 * place_ref[2] + place_ref[1] // 2, r)]


def x_kernel(pieces, swap_ref, *refs):
    blocks, refs = refs[: x_radix * pieces], refs[x_radix * pieces :]
    table_in, table_out, move_ref, upper_ref, lower_ref, inv_upper, inv_lower = refs[:7]
    outs, (high, low, held) = refs[7:11], refs[11:]
    rows = blocks[0].shape[1]

    def wide(table, k, part, span):
        values = table[k, part, span, :]
        return jnp.concatenate([values] * (held.shape[2] // lanes), axis=1)

    def read(q, part, span):
        values = [block[part, span, :] for block in blocks[q * pieces : (q + 1) * pieces]]
        return values[0] if pieces == 1 else jnp.concatenate(values, axis=1)

    def actual(k, swaps):
        return k if k % 2 == 0 else lax.bitwise_xor(k, 2 * swaps)

    def gather_rows(step, carry):
        span = pl.ds(pl.multiple_of(step * strip, strip), strip)
        lower_span = pl.ds(pl.multiple_of(step * strip + rows, strip), strip)
        terms = dft4([(read(q, 0, span), read(q, 1, span)) for q in range(x_radix)], -1.0)
        for k in range(x_radix):
            factor = (wide(table_in, k, 0, span), wide(table_in, k, 1, span))
            real, imag = multiply(terms[k], factor)
            goal = actual(k, swap_ref[0])
            high[goal, span, :], low[goal, span, :] = two_parts(real)
            high[goal, lower_span, :], low[goal, lower_span, :] = two_parts(imag)
        return carry

    lax.fori_loop(0, rows // strip, gather_rows, 0)

    def one_block(k, carry):
        values = columns_product(upper_ref, lower_ref, high[k], low[k])
        moved = multiply((values[:rows], values[rows:]), (move_ref[k, 0], move_ref[k, 1]))
        upper, lower = two_parts(jnp.concatenate(moved, axis=0))
        held[k] = columns_product(inv_upper, inv_lower, upper, lower)
        return carry

    lax.fori_loop(0, x_radix, one_block, 0)

    def scatter_rows(step, carry):
        span = pl.ds(pl.multiple_of(step * strip, strip), strip)
        lower_span = pl.ds(pl.multiple_of(step * strip + rows, strip), strip)
        terms = []
        for k in range(x_radix):
            source = actual(k, swap_ref[1])
            factor = (wide(table_out, k, 0, span), -wide(table_out, k, 1, span))
            terms.append(multiply((held[source, span, :], held[source, lower_span, :]), factor))
        terms = dft4(terms, 1.0)
        for q in range(x_radix):
            for part in range(2):
                outs[q][part, span, :] = terms[q][part]
        return carry

    lax.fori_loop(0, rows // strip, scatter_rows, 0)


def whole(array):
    return pl.BlockSpec(array.shape, lambda *step: (0,) * array.ndim)


smem = pl.BlockSpec(memory_space=pltpu.SMEM)
vmem = pl.BlockSpec(memory_space=pltpu.VMEM)
vmem_limit = 40 * 1024 * 1024


def parameters(steps, limit=vmem_limit):
    return pltpu.CompilerParams(
        vmem_limit_bytes=limit, dimension_semantics=("arbitrary",) * steps
    )


def estimate(microseconds):
    return pl.CostEstimate(
        flops=int(microseconds * 1e9), bytes_accessed=int(microseconds * 3e6), transcendentals=0
    )


def origin_rows(field, place, table, matrices):
    parts, freqs, rows, y_cols = field.shape
    width = y_cols // 4
    out = jax.ShapeDtypeStruct((freqs, parts, rows, width), jnp.float32)

    def fixed(array):
        return pl.BlockSpec(array.shape, lambda j, i, place: (0,) * array.ndim)

    return pl.pallas_call(
        origin_kernel,
        grid_spec=pltpu.PrefetchScalarGridSpec(
            num_scalar_prefetch=1,
            grid=(freqs, rows // row_block),
            in_specs=[
                pl.BlockSpec((parts, 1, row_block, y_cols), lambda j, i, place: (0, j, i, 0)),
                fixed(table),
                fixed(matrices[0]),
                fixed(matrices[1]),
            ],
            out_specs=[
                pl.BlockSpec(
                    (1, parts, row_block, width),
                    lambda j, i, place: (lax.bitwise_xor(j, place[1] // 2), 0, i, 0),
                )
            ]
            * 4,
        ),
        out_shape=[out] * 4,
        compiler_params=parameters(2, 60 * 1024 * 1024),
        cost_estimate=estimate(6),
        name="origin_rows",
    )(place, field, table, *matrices)


def turn_rows(keeps_field, depth_step, slot, scale, blocks, screen, table, inverse, forward):
    parts, rows, width = blocks[0].shape
    y_cols = screen.shape[0] * screen.shape[-1]
    block = pl.BlockSpec((parts, row_block, width), lambda i: (0, i, 0))
    full = pl.BlockSpec((parts, row_block, y_cols), lambda i: (0, i, 0))
    out = [jax.ShapeDtypeStruct((parts, rows, width), jnp.float32)] * 4
    out_specs = [block] * 4
    if keeps_field:
        out = out + [jax.ShapeDtypeStruct((parts, rows, y_cols), jnp.float32)]
        out_specs = out_specs + [full]
    return pl.pallas_call(
        functools.partial(turn_kernel, keeps_field),
        grid=(rows // row_block,),
        in_specs=[smem]
        + [block] * 4
        + [pl.BlockSpec((4, 1, 1, row_block, width), lambda i: (0, depth_step, slot, i, 0))]
        + [whole(array) for array in (table, *inverse, *forward)],
        out_specs=out_specs,
        out_shape=out,
        compiler_params=parameters(1),
        cost_estimate=estimate(5),
        name="turn_rows",
    )(scale, *blocks, screen, table, *inverse, *forward)


def image_rows(depth_step, place, scale, own, blocks, screen, table, inverse):
    parts, rows, width = blocks[0].shape
    y_cols = screen.shape[0] * screen.shape[-1]
    own_ready = len(own) == 1
    block = pl.BlockSpec((parts, row_block, width), lambda i: (0, i, 0))
    full = pl.BlockSpec((parts, row_block, y_cols), lambda i: (0, i, 0))
    return pl.pallas_call(
        functools.partial(image_kernel, own_ready),
        grid=(rows // row_block,),
        in_specs=[smem, smem]
        + ([full] if own_ready else [block] * 4)
        + [block] * 4
        + [pl.BlockSpec((4, 1, 1, row_block, width), lambda i: (0, depth_step, 0, i, 0))]
        + [whole(array) for array in (table, *inverse)],
        out_specs=[pl.BlockSpec((row_block, width), lambda i: (i, 0))] * 4,
        out_shape=[jax.ShapeDtypeStruct((rows, width), jnp.float32)] * 4,
        scratch_shapes=[pltpu.VMEM((4, row_block, width), jnp.float32)],
        compiler_params=parameters(1),
        cost_estimate=estimate(4),
        name="image_rows",
    )(place, scale, *own, *blocks, screen, table, *inverse)


def move_columns(chunk, swaps, blocks, table_in, table_out, move, forward, inverse):
    pieces = len(blocks[0])
    parts, rows, width = blocks[0][0].shape
    width = pieces * width
    move_block = pl.BlockSpec((x_radix, parts, rows, width), lambda i: (0, 0, 0, chunk))
    blocks = [piece for block in blocks for piece in block]
    block = pl.BlockSpec((parts, rows, width), lambda i: (0, 0, 0))
    return pl.pallas_call(
        functools.partial(x_kernel, pieces),
        grid=(1,),
        in_specs=[smem] + [whole(piece) for piece in blocks] + [whole(table_in), whole(table_out), move_block]
        + [whole(array) for array in (*forward, *inverse)],
        out_specs=[block] * 4,
        out_shape=[jax.ShapeDtypeStruct((parts, rows, width), jnp.float32)] * 4,
        scratch_shapes=[
            pltpu.VMEM((x_radix, parts * rows, width), jnp.bfloat16),
            pltpu.VMEM((x_radix, parts * rows, width), jnp.bfloat16),
            pltpu.VMEM((x_radix, parts * rows, width), jnp.float32),
        ],
        compiler_params=parameters(1),
        cost_estimate=estimate(8),
        name="move_columns",
    )(swaps, *blocks, table_in, table_out, move, *forward, *inverse)


def y_table(core, y_cols):
    k = (jnp.arange(y_radix, dtype=jnp.int32) ^ (4 * core))[:, None]
    r = jnp.arange(lanes, dtype=jnp.int32)[None, :]
    angles = 2.0 * math.pi / y_cols * (k * r % y_cols).astype(jnp.float32)
    return jnp.stack([jnp.cos(angles), -jnp.sin(angles)], axis=1)


def x_table(order, x_total):
    rows = x_total // x_radix
    low_bit, high_bit = order & 1, order >> 1
    slot = jnp.arange(x_radix, dtype=jnp.int32)
    k = jnp.where(slot % 2 == 1, slot ^ (2 * low_bit), slot)
    eighths = jnp.where(k % 2 == 1, 4 * high_bit, 0)
    turns = jnp.array([0, 6, 4, 2], jnp.int32)
    eighths = eighths + low_bit * turns[k]
    row = jnp.arange(rows, dtype=jnp.int32)[None, :]
    steps = (x_total // 8 * eighths[:, None] - k[:, None] * row) % x_total
    angles = 2.0 * math.pi / x_total * steps.astype(jnp.float32)
    table = jnp.stack([jnp.cos(angles), jnp.sin(angles)], axis=1)
    return jnp.broadcast_to(table[..., None], table.shape + (lanes,))


def move_table(omega, polarity, core, x_total, y_total):
    k = jnp.arange(x_radix, dtype=jnp.int32)[:, None]
    inner = jnp.arange(x_total // x_radix, dtype=jnp.int32)[None, :]
    x_waves = wave_number(k + x_radix * inner, x_total)
    ky = jnp.arange(y_radix // 2, dtype=jnp.int32)[:, None] + y_radix // 2 * core
    inner = jnp.arange(lanes, dtype=jnp.int32)[None, :]
    y_waves = wave_number((ky + y_radix * inner).reshape(-1), y_total)
    lateral = x_waves[:, :, None] ** 2 + y_waves[None, None, :] ** 2
    kz_square = (omega * reference_slowness) ** 2 - lateral
    kz_root = jnp.sqrt(jnp.abs(kz_square))
    travels = kz_square >= 0.0
    amplitude = jnp.where(travels, 1.0, jnp.exp(-kz_root * depth_interval))
    amplitude = amplitude / (x_total * y_total)
    angles = jnp.where(travels, polarity * kz_root * depth_interval, 0.0)
    return jnp.stack([amplitude * jnp.cos(angles), amplitude * jnp.sin(angles)], axis=1)


def zero_after(*others):
    corners = sum(other[(0,) * other.ndim] for other in others)
    return (corners * 0.0).astype(jnp.int32)


def per_device_fields(sizes, wavefields, slowness, freq_index):
    s, z, x, c = (lax.axis_index(axis) for axis in axes)
    rows, y_cols = wavefields.shape[3:]
    x_total = rows * sizes["gy"]
    place = jnp.stack([s, z, x, c]).astype(jnp.int32)

    def send(array, target):
        return lax.ppermute(array, axes, route(sizes, target))

    def to_core(array):
        return send(array, lambda s, z, x, c: (s, z, x, 1 - c))

    def to_partner(array):
        return send(array, lambda s, z, x, c: (s, z ^ 1, x, c))

    def to_partner_core(array):
        return send(array, lambda s, z, x, c: (s, z ^ 1, x, 1 - c))

    def to_freq(array):
        return send(array, lambda s, z, x, c: (s, z, 1 - x, c))

    def to_shot(array):
        return send(array, lambda s, z, x, c: (1 - s, z, x, c))

    def along_z(array, r):
        return send(array, lambda s, z, x, c: (s, z ^ r, x, c))

    row_forward = row_matrix(lanes, -1.0)
    row_inverse = row_matrix(lanes, 1.0)
    column_forward = column_matrix(rows, -1.0)
    column_inverse = column_matrix(rows, 1.0)

    width = y_cols // 8
    piece = lax.dynamic_slice_in_dim(slowness, (4 * s + 2 * x + c) * width, width, 2)
    pieces = [piece] + [along_z(piece, r) for r in (2, 3, 1)]

    def all_columns(late):
        stacked = jnp.stack([pieces[k] for k in (0, 3, 1, 2)], axis=1)
        mine = lax.dynamic_slice_in_dim(stacked, 2 * ((z // 2) ^ c) + late, 2, 1)
        theirs = to_core(
            lax.dynamic_slice_in_dim(stacked, 2 * ((z // 2) ^ (1 - c)) + late, 2, 1)
        )
        both = jnp.where(
            c == 0, jnp.concatenate([mine, theirs], 3), jnp.concatenate([theirs, mine], 3)
        )
        other = to_freq(both)
        pair = jnp.where(x == 0, jnp.stack([both, other]), jnp.stack([other, both]))
        far = to_shot(pair)
        return jnp.where(s == 0, jnp.concatenate([pair, far]), jnp.concatenate([far, pair]))

    y_steps = y_table(c, y_cols)
    spectra = origin_rows(wavefields[0], place, y_steps, row_forward)
    kept_is_odd = (z ^ c) % 2 == 1
    arrived = []
    for chunk in range(2):
        kept, crossed = spectra[chunk], to_core(spectra[2 + chunk])
        even = jnp.where(kept_is_odd, crossed, kept)
        odd = jnp.where(kept_is_odd, kept, crossed)
        far = along_z(even[1], 2)
        farthest = along_z(odd[1], 3)
        arrived.append([[even[0]], [along_z(odd[0], 1)], [far], [farthest]])

    late = zero_after(arrived[0][1][0])
    layers = all_columns(late)

    z_late = z + late
    side = z_late % 2
    index = lax.dynamic_index_in_dim(freq_index, z_late // 2, 0, keepdims=False)
    omega = omega_unit * index.astype(jnp.float32)
    polarity = (2 * side - 1).astype(jnp.float32)
    order = 2 * c + side
    move = move_table(omega, polarity, c, x_total, y_cols)
    table_z = x_table(z_late, x_total)
    table_order = x_table(order, x_total)
    scale = (polarity * omega).reshape(1)

    images = []
    blocks_in, order_in, table_in, hold = arrived, z, table_z, 0
    for depth_step in range(DEPTH):
        last = depth_step == DEPTH - 1
        swaps = jnp.stack([order_in & 1, order & 1]).astype(jnp.int32) + hold
        near, partner = [], []
        for chunk in range(2):
            out = move_columns(
                chunk, swaps, blocks_in[chunk], table_in, table_order, move,
                column_forward, column_inverse,
            )
            crossed = [to_core(out[2]), None if last else to_core(out[3])]
            near.append([[out[0], crossed[0]], [out[1], crossed[1]]])
            partner.append([to_partner(out[1]), to_partner_core(out[3])])

        def y_blocks(pairs):
            return [pairs[0][0], pairs[1][0], pairs[0][1], pairs[1][1]]

        own = y_blocks([near[0][0], near[1][0]])
        far_blocks = y_blocks(partner)
        if not last:
            turned = [None, None]
            waits = [zero_after(*partner[0]).astype(jnp.float32), 0.0]
            for slot in (1, 0):
                blocks = y_blocks([near[0][slot], near[1][slot]])
                turned[slot] = turn_rows(
                    slot == 0, depth_step, slot, scale + waits[slot], blocks, layers, y_steps,
                    row_inverse, row_forward,
                )
            blocks_in = [
                [
                    [turned[0][k]],
                    [turned[1][k]],
                    [to_core(turned[0][2 + k])],
                    [to_core(turned[1][2 + k])],
                ]
                for k in range(2)
            ]
            hold = zero_after(*partner[1])
            order_in, table_in = order, table_order
            own = [turned[0][4]]
        terms = image_rows(
            depth_step, place, scale, own, far_blocks, layers, y_steps, row_inverse
        )

        def gather(r):
            def target(s, z, x, c):
                quarter = (2 * x + z // 2) ^ r
                return s, 2 * c + z % 2, quarter // 2, quarter % 2

            return send(terms[r], target)

        images.append(sum(gather(r) for r in range(4)))
    return jnp.stack(images)


def solution(mesh):
    sizes = dict(mesh.shape)

    def per_device(wavefields, slowness, freq_index):
        if fits_one_field_per_chip(sizes, wavefields.shape):
            return per_device_fields(sizes, wavefields, slowness, freq_index)
        return per_device_pencils(wavefields, slowness, freq_index)

    placed = (P("fld", None, ("shot", "freq"), "gy", None), P(None, "gy", None), P("freq"))
    return jax.shard_map(
        per_device,
        mesh=mesh,
        in_specs=placed,
        out_specs=P("shot", "gy", ("freq", "fld")),
        check_vma=False,
    )
```

```python
import functools
import math

import jax
import jax.numpy as jnp
import numpy as np
from jax import lax
from jax.experimental import pallas as pl
from jax.experimental.pallas import tpu as pltpu
from jax.sharding import PartitionSpec as P

DEPTH = 2


omega_unit = 0.1
reference_slowness = 1.0
depth_interval = 1.0
inner_length = 128


def contract(pattern, values, matrix):
    return jnp.einsum(
        pattern, values, matrix, precision=lax.Precision.HIGHEST, preferred_element_type=jnp.float32
    )


def complex_table(length, polarity):
    indices = jnp.arange(length, dtype=jnp.int32)
    angles = (
        2.0 * math.pi / length * (indices[:, None] * indices[None, :] % length).astype(jnp.float32)
    )
    cosine = jnp.cos(angles)
    sine_part = polarity * jnp.sin(angles)
    upper = jnp.stack([cosine, sine_part], axis=1)
    lower = jnp.stack([-sine_part, cosine], axis=1)
    return jnp.stack([upper, lower], axis=0)


def twiddle(outer_size, inner_size, length, polarity):
    outer_index = jnp.arange(outer_size, dtype=jnp.int32)[:, None]
    inner_index = jnp.arange(inner_size, dtype=jnp.int32)[None, :]
    angles = 2.0 * math.pi / length * (outer_index * inner_index % length).astype(jnp.float32)
    return (jnp.cos(angles), polarity * jnp.sin(angles))


def rotate(values, cosine, sine_part):
    real_part = values[0]
    imag_part = values[1]
    return jnp.stack(
        [real_part * cosine - imag_part * sine_part, real_part * sine_part + imag_part * cosine]
    )


def wave_number(indices, length):
    signed = jnp.where(indices < length // 2, indices, indices - length)
    return 2.0 * math.pi / length * signed.astype(jnp.float32)


def forward_rows(wave_field):
    batches, x_rows, y_cols = wave_field.shape[1:]
    outer_size = y_cols // inner_length
    blocks = wave_field.reshape(2, batches, x_rows, outer_size, inner_length)
    blocks = contract("cbxan,cadk->dbxkn", blocks, complex_table(outer_size, -1.0))
    cosine, sine_part = twiddle(outer_size, inner_length, y_cols, -1.0)
    blocks = rotate(blocks, cosine, sine_part)
    blocks = contract("cbxkn,cndm->dbxkm", blocks, complex_table(inner_length, -1.0))
    return blocks.reshape(2, batches, x_rows, y_cols)


def inverse_rows(wave_field):
    batches, x_rows, y_cols = wave_field.shape[1:]
    outer_size = y_cols // inner_length
    blocks = wave_field.reshape(2, batches, x_rows, outer_size, inner_length)
    blocks = contract("cbxkm,cmdn->dbxkn", blocks, complex_table(inner_length, 1.0))
    cosine, sine_part = twiddle(outer_size, inner_length, y_cols, 1.0)
    blocks = rotate(blocks, cosine, sine_part)
    blocks = contract("cbxkn,ckda->dbxan", blocks, complex_table(outer_size, 1.0))
    return blocks.reshape(2, batches, x_rows, y_cols) / y_cols


def forward_columns(blocks):
    inner_size = blocks.shape[2]
    pencils = blocks.shape[3]
    blocks = contract("cbnsy,csdk->dbnky", blocks, complex_table(pencils, -1.0))
    cosine, sine_part = twiddle(pencils, inner_size, inner_size * pencils, -1.0)
    blocks = rotate(blocks, cosine.T[:, :, None], sine_part.T[:, :, None])
    return contract("cbnky,cndm->dbmky", blocks, complex_table(inner_size, -1.0))


def inverse_columns(blocks):
    inner_size = blocks.shape[2]
    pencils = blocks.shape[3]
    blocks = contract("cbmky,cmdn->dbnky", blocks, complex_table(inner_size, 1.0))
    cosine, sine_part = twiddle(pencils, inner_size, inner_size * pencils, 1.0)
    blocks = rotate(blocks, cosine.T[:, :, None], sine_part.T[:, :, None])
    blocks = contract("cbnky,ckds->dbnsy", blocks, complex_table(pencils, 1.0))
    return blocks / (inner_size * pencils)


def propagate(blocks, omegas, polarities, y_total):
    inner_size, pencils, y_local = blocks.shape[2:]
    x_index = (
        jnp.arange(pencils, dtype=jnp.int32)[None, :]
        + pencils * jnp.arange(inner_size, dtype=jnp.int32)[:, None]
    )
    stored = lax.axis_index("gy") * y_local + jnp.arange(y_local, dtype=jnp.int32)
    y_index = stored // inner_length + y_total // inner_length * (stored % inner_length)
    x_waves = wave_number(x_index, inner_size * pencils)
    y_waves = wave_number(y_index, y_total)
    lateral = x_waves[:, :, None] ** 2 + y_waves[None, None, :] ** 2
    kz_square = ((omegas * reference_slowness) ** 2)[:, None, None, None] - lateral[None]
    kz_root = jnp.sqrt(jnp.abs(kz_square))
    travels = kz_square >= 0.0
    amplitude = jnp.where(travels, 1.0, jnp.exp(-kz_root * depth_interval))
    angles = jnp.where(travels, polarities[:, None, None, None] * kz_root * depth_interval, 0.0)
    return rotate(blocks, amplitude * jnp.cos(angles), amplitude * jnp.sin(angles))


def apply_screen(wave_field, slowness_now, omegas, polarities):
    phases = (polarities * omegas)[:, None, None] * (
        (slowness_now - reference_slowness) * depth_interval
    )[None]
    return rotate(wave_field, jnp.cos(phases), jnp.sin(phases))


def per_device_pencils(wavefields, slowness, freq_index):
    x_rows = wavefields.shape[3]
    y_cols = wavefields.shape[4]
    pencils = lax.axis_size("gy")
    freq_devs = lax.axis_size("freq")
    fld_devs = lax.axis_size("fld")
    column_width = y_cols // (freq_devs * fld_devs)
    omegas = omega_unit * freq_index.astype(jnp.float32)
    per_side = wavefields.shape[2] // fld_devs
    regrouped = wavefields.reshape(2, 1, fld_devs, per_side, x_rows, y_cols)
    paired = lax.all_to_all(regrouped, "fld", split_axis=2, concat_axis=1, tiled=True)
    wave_field = paired.reshape(2, fld_devs * per_side, x_rows, y_cols)
    local_omegas = lax.dynamic_slice_in_dim(omegas, lax.axis_index("fld") * per_side, per_side)
    omegas = jnp.tile(local_omegas, fld_devs)
    polarities = jnp.repeat(jnp.array([-1.0, 1.0], jnp.float32), per_side)
    batches = wave_field.shape[1]
    images = []
    for depth_step in range(DEPTH):
        wave_field = forward_rows(wave_field)
        blocks = wave_field.reshape(2, batches, x_rows, pencils, y_cols // pencils)
        blocks = lax.all_to_all(blocks, "gy", split_axis=3, concat_axis=3, tiled=True)
        blocks = forward_columns(blocks)
        blocks = propagate(blocks, omegas, polarities, y_cols)
        blocks = inverse_columns(blocks)
        blocks = lax.all_to_all(blocks, "gy", split_axis=3, concat_axis=3, tiled=True)
        wave_field = inverse_rows(blocks.reshape(2, batches, x_rows, y_cols))
        wave_field = apply_screen(wave_field, slowness[depth_step], omegas, polarities)
        source = wave_field[:, :per_side]
        receiver = wave_field[:, per_side:]
        summed = jnp.sum(source[0] * receiver[0] + source[1] * receiver[1], axis=0)
        partial_image = summed.reshape(x_rows, freq_devs * fld_devs, column_width)[None]
        images.append(
            lax.psum_scatter(partial_image, ("freq", "fld"), scatter_dimension=2, tiled=True)
        )
    combined = jnp.concatenate(images, axis=0)
    return combined.reshape(DEPTH, x_rows, column_width)


axes = ("shot", "gy", "freq", "fld")
lanes = 128
y_radix = 8
x_radix = 4
row_group = 32
strip = 16


def fits_one_field_per_chip(sizes, shape):
    return (
        sizes["gy"] == 4
        and sizes["freq"] == 2
        and sizes["fld"] == 2
        and shape[2] == 2
        and shape[4] == y_radix * lanes
        and shape[3] % row_group == 0
        and shape[3] * 4 == shape[4]
    )


def route(sizes, target):
    pairs = []
    for place in np.ndindex(*(sizes[axis] for axis in axes)):
        goal = target(*place)
        if goal is not None:
            dims = tuple(sizes[axis] for axis in axes)
            pairs.append(
                (int(np.ravel_multi_index(place, dims)), int(np.ravel_multi_index(goal, dims)))
            )
    return pairs


def split_constant(matrix):
    upper = matrix.astype(jnp.bfloat16)
    lower = (matrix - upper.astype(np.float64)).astype(jnp.bfloat16)
    return upper, lower


def dft_parts(length, polarity):
    indices = np.arange(length)
    angles = 2.0 * np.pi / length * (indices[:, None] * indices[None, :] % length)
    return np.cos(angles), polarity * np.sin(angles)


def row_matrix(length, polarity):
    cosine, sine = dft_parts(length, polarity)
    return split_constant(np.block([[cosine, sine], [-sine, cosine]]))


def column_matrix(length, polarity):
    cosine, sine = dft_parts(length, polarity)
    return split_constant(np.block([[cosine, -sine], [sine, cosine]]))


def add(one, two):
    return one[0] + two[0], one[1] + two[1]


def subtract(one, two):
    return one[0] - two[0], one[1] - two[1]


def multiply(one, two):
    return one[0] * two[0] - one[1] * two[1], one[0] * two[1] + one[1] * two[0]


def conjugate(one):
    return one[0], -one[1]


def quarter_turn(one, polarity):
    if polarity > 0:
        return -one[1], one[0]
    return one[1], -one[0]


def dft4(terms, polarity):
    even = add(terms[0], terms[2])
    odd = subtract(terms[0], terms[2])
    even_other = add(terms[1], terms[3])
    odd_other = quarter_turn(subtract(terms[1], terms[3]), polarity)
    return [
        add(even, even_other),
        add(odd, odd_other),
        subtract(even, even_other),
        subtract(odd, odd_other),
    ]


def eighth_turn(one, polarity):
    half = math.sqrt(0.5)
    if polarity > 0:
        return (one[0] - one[1]) * half, (one[0] + one[1]) * half
    return (one[0] + one[1]) * half, (one[1] - one[0]) * half


def dft8(terms, polarity):
    sums = [add(terms[a], terms[a + 4]) for a in range(4)]
    differences = [subtract(terms[a], terms[a + 4]) for a in range(4)]
    turned = [
        differences[0],
        eighth_turn(differences[1], polarity),
        quarter_turn(differences[2], polarity),
        quarter_turn(eighth_turn(differences[3], polarity), polarity),
    ]
    even = dft4(sums, polarity)
    odd = dft4(turned, polarity)
    return [even[k // 2] if k % 2 == 0 else odd[k // 2] for k in range(8)]


def two_parts(values):
    upper = values.astype(jnp.bfloat16)
    lower = (values - upper.astype(jnp.float32)).astype(jnp.bfloat16)
    return upper, lower


def dot(left, right):
    return jnp.dot(left, right, preferred_element_type=jnp.float32)


def rows_product(values, upper_ref, lower_ref):
    upper, lower = two_parts(values)
    return dot(upper, upper_ref[...]) + dot(lower, upper_ref[...]) + dot(upper, lower_ref[...])


def columns_product(upper_ref, lower_ref, upper, lower):
    return dot(upper_ref[...], upper) + dot(upper_ref[...], lower) + dot(lower_ref[...], upper)


def stack_blocks(terms):
    return jnp.concatenate([jnp.concatenate(term, axis=1) for term in terms], axis=0)


def unstack_blocks(values, rows):
    blocks = [values[k * rows : (k + 1) * rows] for k in range(y_radix)]
    return [(block[:, :lanes], block[:, lanes:]) for block in blocks]


def y_twiddle(table_ref, k):
    return table_ref[k, 0:1, :], table_ref[k, 1:2, :]


def forward_y(terms, table_ref, upper_ref, lower_ref):
    rows = terms[0][0].shape[0]
    turned = dft8(terms, -1.0)
    turned = [multiply(turned[k], y_twiddle(table_ref, k)) for k in range(y_radix)]
    return unstack_blocks(rows_product(stack_blocks(turned), upper_ref, lower_ref), rows)


def inverse_y(terms, table_ref, upper_ref, lower_ref):
    rows = terms[0][0].shape[0]
    inner = unstack_blocks(rows_product(stack_blocks(terms), upper_ref, lower_ref), rows)
    inner = [multiply(inner[k], conjugate(y_twiddle(table_ref, k))) for k in range(y_radix)]
    return dft8(inner, 1.0)


def lane_block(index):
    return slice(index * lanes, (index + 1) * lanes)


def row_groups(rows):
    return [slice(first, first + row_group) for first in range(0, rows, row_group)]


def origin_kernel(place_ref, field_ref, table_ref, upper_ref, lower_ref, *outs):
    sign = (1 - 2 * place_ref[3]).astype(jnp.float32)
    for rows in row_groups(field_ref.shape[2]):
        terms = []
        for a in range(y_radix):
            term = (field_ref[0, 0, rows, lane_block(a)], field_ref[1, 0, rows, lane_block(a)])
            terms.append((term[0] * sign, term[1] * sign) if a % 2 else term)
        spectrum = forward_y(terms, table_ref, upper_ref, lower_ref)
        for k in range(y_radix):
            for part in range(2):
                outs[k // 2][0, part, rows, lane_block(k % 2)] = spectrum[k][part]


def read_y_blocks(blocks, rows):
    return [
        tuple(blocks[k // 2][part, rows, lane_block(k % 2)] for part in range(2))
        for k in range(y_radix)
    ]


def read_layer(ref, at, rows):
    return [ref[a // 2, at[0], at[1], rows, lane_block(a % 2)] for a in range(y_radix)]


def screen_of(scale_ref, layer):
    phase = scale_ref[0] * ((layer - reference_slowness) * depth_interval)
    square = phase * phase
    cosine, sine = 1.0 / 40320.0, 1.0 / 362880.0
    for term in (-1.0 / 720.0, 1.0 / 24.0, -0.5, 1.0):
        cosine = cosine * square + term
    for term in (-1.0 / 5040.0, 1.0 / 120.0, -1.0 / 6.0, 1.0):
        sine = sine * square + term
    return cosine, sine * phase


def turn_kernel(keeps_field, at, scale_ref, *refs):
    blocks, layer_ref, refs = refs[:4], refs[4], refs[5:]
    table_ref, inv_upper, inv_lower, upper_ref, lower_ref = refs[:5]
    outs = refs[5:]
    for rows in row_groups(blocks[0].shape[1]):
        terms = inverse_y(read_y_blocks(blocks, rows), table_ref, inv_upper, inv_lower)
        layer = read_layer(layer_ref, at, rows)
        terms = [multiply(terms[a], screen_of(scale_ref, layer[a])) for a in range(y_radix)]
        if keeps_field:
            for a in range(y_radix):
                for part in range(2):
                    outs[4][part, rows, lane_block(a)] = terms[a][part]
        spectrum = forward_y(terms, table_ref, upper_ref, lower_ref)
        for k in range(y_radix):
            for part in range(2):
                outs[k // 2][part, rows, lane_block(k % 2)] = spectrum[k][part]


def image_kernel(own_ready, at, place_ref, scale_ref, *refs):
    own_count = 1 if own_ready else 4
    own, refs = refs[:own_count], refs[own_count:]
    blocks, layer_ref, refs = refs[:4], refs[4], refs[5:]
    table_ref, inv_upper, inv_lower = refs[:3]
    outs, quarters = refs[3:7], refs[7]
    for rows in row_groups(blocks[0].shape[1]):
        layer = read_layer(layer_ref, at, rows)
        other = inverse_y(read_y_blocks(blocks, rows), table_ref, inv_upper, inv_lower)
        if not own_ready:
            mine = inverse_y(read_y_blocks(own, rows), table_ref, inv_upper, inv_lower)
        for a in range(y_radix):
            screen = screen_of(scale_ref, layer[a])
            if own_ready:
                near = (own[0][0, rows, lane_block(a)], own[0][1, rows, lane_block(a)])
            else:
                near = multiply(mine[a], screen)
            far = multiply(other[a], conjugate(screen))
            quarters[a // 2, rows, lane_block(a % 2)] = near[0] * far[0] + near[1] * far[1]
    for r in range(4):
        outs[r][...] = quarters[lax.bitwise_xor(2 * place_ref[2] + place_ref[1] // 2, r)]


def x_kernel(swap_ref, *refs):
    blocks, refs = refs[:x_radix], refs[x_radix:]
    table_in, table_out, half_ref, move_ref, upper_ref, lower_ref, inv_upper, inv_lower = refs[:8]
    outs, (high, low, held) = refs[8:12], refs[12:]
    inner = blocks[0].shape[1] // 2

    def wide(table, *at):
        values = table[at]
        return jnp.concatenate([values] * (held.shape[2] // lanes), axis=1)

    def actual(k, swaps):
        return k if k % 2 == 0 else lax.bitwise_xor(k, 2 * swaps)

    def spans(step):
        first = pl.multiple_of(step * strip, strip)
        return pl.ds(first, strip), pl.ds(pl.multiple_of(first + inner, strip), strip)

    def gather_rows(step, carry):
        span, second = spans(step)
        halves = []
        for rows in (span, second):
            terms = dft4([(block[0, rows, :], block[1, rows, :]) for block in blocks], -1.0)
            halves.append(
                [
                    multiply(terms[k], (wide(table_in, k, 0, rows), wide(table_in, k, 1, rows)))
                    for k in range(x_radix)
                ]
            )
        turn = (wide(half_ref, 0, span), wide(half_ref, 1, span))
        for k in range(x_radix):
            goal = 2 * actual(k, swap_ref[0])
            pair = (
                add(halves[0][k], halves[1][k]),
                multiply(subtract(halves[0][k], halves[1][k]), turn),
            )
            for e in range(2):
                high[goal + e, span, :], low[goal + e, span, :] = two_parts(pair[e][0])
                high[goal + e, second, :], low[goal + e, second, :] = two_parts(pair[e][1])
        return carry

    lax.fori_loop(0, inner // strip, gather_rows, 0, unroll=2)

    for k in range(2 * x_radix):
        values = columns_product(upper_ref, lower_ref, high[k], low[k])
        moved = multiply((values[:inner], values[inner:]), (move_ref[k, 0], move_ref[k, 1]))
        upper, lower = two_parts(jnp.concatenate(moved, axis=0))
        held[k] = columns_product(inv_upper, inv_lower, upper, lower)

    def scatter_rows(step, carry):
        span, second = spans(step)
        turn = (wide(half_ref, 0, span), -wide(half_ref, 1, span))
        halves = [[], []]
        for k in range(x_radix):
            source = 2 * actual(k, swap_ref[1])
            even = (held[source, span, :], held[source, second, :])
            odd = multiply((held[source + 1, span, :], held[source + 1, second, :]), turn)
            for half, rows, term in ((0, span, add(even, odd)), (1, second, subtract(even, odd))):
                factor = (wide(table_out, k, 0, rows), -wide(table_out, k, 1, rows))
                halves[half].append(multiply(term, factor))
        for half, rows in ((0, span), (1, second)):
            terms = dft4(halves[half], 1.0)
            for q in range(x_radix):
                for part in range(2):
                    outs[q][part, rows, :] = terms[q][part]
        return carry

    lax.fori_loop(0, inner // strip, scatter_rows, 0, unroll=2)


smem = pl.BlockSpec(memory_space=pltpu.SMEM)
vmem = pl.BlockSpec(memory_space=pltpu.VMEM)
column_limit = 24 * 1024 * 1024
row_limit = 24 * 1024 * 1024


def estimate(microseconds):
    return pl.CostEstimate(
        flops=int(microseconds * 1e9), bytes_accessed=int(microseconds * 3e6), transcendentals=0
    )


def origin_rows(field, place, table, matrices):
    parts, freqs, rows, y_cols = field.shape
    width = y_cols // 4
    out = jax.ShapeDtypeStruct((freqs, parts, rows, width), jnp.float32)

    def fixed(array):
        return pl.BlockSpec(array.shape, lambda j, place: (0,) * array.ndim)

    return pl.pallas_call(
        origin_kernel,
        grid_spec=pltpu.PrefetchScalarGridSpec(
            num_scalar_prefetch=1,
            grid=(freqs,),
            in_specs=[
                pl.BlockSpec((parts, 1, rows, y_cols), lambda j, place: (0, j, 0, 0)),
                fixed(table),
                fixed(matrices[0]),
                fixed(matrices[1]),
            ],
            out_specs=[
                pl.BlockSpec(
                    (1, parts, rows, width),
                    lambda j, place: (lax.bitwise_xor(j, place[1] // 2), 0, 0, 0),
                )
            ]
            * 4,
        ),
        out_shape=[out] * 4,
        compiler_params=pltpu.CompilerParams(
            vmem_limit_bytes=60 * 1024 * 1024, dimension_semantics=("arbitrary",)
        ),
        cost_estimate=estimate(6),
        name="origin_rows",
    )(place, field, table, *matrices)


def turn_rows(keeps_field, at, scale, blocks, layers, table, inverse, forward):
    parts, rows, width = blocks[0].shape
    out = [jax.ShapeDtypeStruct((parts, rows, width), jnp.float32)] * 4
    if keeps_field:
        out = out + [jax.ShapeDtypeStruct((parts, rows, 4 * width), jnp.float32)]
    return pl.pallas_call(
        functools.partial(turn_kernel, keeps_field, at),
        in_specs=[smem] + [vmem] * 10,
        out_specs=[vmem] * len(out),
        out_shape=out,
        compiler_params=pltpu.CompilerParams(vmem_limit_bytes=row_limit),
        cost_estimate=estimate(4),
        name="turn_rows",
    )(scale, *blocks, layers, table, *inverse, *forward)


def image_rows(at, place, scale, own, blocks, layers, table, inverse):
    parts, rows, width = blocks[0].shape
    return pl.pallas_call(
        functools.partial(image_kernel, len(own) == 1, at),
        in_specs=[smem, smem] + [vmem] * (len(own) + 8),
        out_specs=[vmem] * 4,
        out_shape=[jax.ShapeDtypeStruct((rows, width), jnp.float32)] * 4,
        scratch_shapes=[pltpu.VMEM((4, rows, width), jnp.float32)],
        compiler_params=pltpu.CompilerParams(vmem_limit_bytes=row_limit),
        cost_estimate=estimate(3),
        name="image_rows",
    )(place, scale, *own, *blocks, layers, table, *inverse)


def move_columns(swaps, blocks, tables, move, forward, inverse):
    parts, rows, width = blocks[0].shape
    inner = parts * rows // 2
    return pl.pallas_call(
        x_kernel,
        in_specs=[smem] + [vmem] * (x_radix + 8),
        out_specs=[vmem] * x_radix,
        out_shape=[jax.ShapeDtypeStruct((parts, rows, width), jnp.float32)] * x_radix,
        scratch_shapes=[
            pltpu.VMEM((2 * x_radix, inner, width), jnp.bfloat16),
            pltpu.VMEM((2 * x_radix, inner, width), jnp.bfloat16),
            pltpu.VMEM((2 * x_radix, inner, width), jnp.float32),
        ],
        compiler_params=pltpu.CompilerParams(vmem_limit_bytes=column_limit),
        cost_estimate=estimate(6),
        name="move_columns",
    )(swaps, *blocks, *tables, move, *forward, *inverse)


def y_table(core, y_cols):
    k = (jnp.arange(y_radix, dtype=jnp.int32) ^ (4 * core))[:, None]
    r = jnp.arange(lanes, dtype=jnp.int32)[None, :]
    angles = 2.0 * math.pi / y_cols * (k * r % y_cols).astype(jnp.float32)
    return jnp.stack([jnp.cos(angles), -jnp.sin(angles)], axis=1)


def x_table(order, x_total):
    rows = x_total // x_radix
    low_bit, high_bit = order & 1, order >> 1
    slot = jnp.arange(x_radix, dtype=jnp.int32)
    k = jnp.where(slot % 2 == 1, slot ^ (2 * low_bit), slot)
    eighths = jnp.where(k % 2 == 1, 4 * high_bit, 0)
    turns = jnp.array([0, 6, 4, 2], jnp.int32)
    eighths = eighths + low_bit * turns[k]
    row = jnp.arange(rows, dtype=jnp.int32)[None, :]
    steps = (x_total // 8 * eighths[:, None] - k[:, None] * row) % x_total
    angles = 2.0 * math.pi / x_total * steps.astype(jnp.float32)
    table = jnp.stack([jnp.cos(angles), jnp.sin(angles)], axis=1)
    return jnp.broadcast_to(table[..., None], table.shape + (lanes,))


def cosine_sine(angles):
    half = 0.5 * angles
    square = half * half
    cosine, sine = 1.0 / math.factorial(12), -1.0 / math.factorial(11)
    for order in (10, 8, 6, 4, 2, 0):
        sign = -1.0 if order % 4 else 1.0
        cosine = cosine * square + sign / math.factorial(order)
        if order:
            sine = sine * square - sign / math.factorial(order - 1)
    sine = sine * half
    return 1.0 - 2.0 * sine * sine, 2.0 * sine * cosine


def half_table(rows):
    angles = -2.0 * np.pi / rows * np.arange(rows // 2)
    table = np.stack([np.cos(angles), np.sin(angles)]).astype(np.float32)
    return jnp.asarray(np.ascontiguousarray(np.broadcast_to(table[..., None], table.shape + (lanes,))))


def move_table(chunk, omega, polarity, core, x_total, y_total):
    step = jnp.arange(2 * x_radix, dtype=jnp.int32)[:, None]
    inner = jnp.arange(x_total // (2 * x_radix), dtype=jnp.int32)[None, :]
    x_waves = wave_number(step // 2 + x_radix * (2 * inner + step % 2), x_total)
    ky = jnp.arange(2, dtype=jnp.int32)[:, None] + 2 * chunk + y_radix // 2 * core
    inner = jnp.arange(lanes, dtype=jnp.int32)[None, :]
    y_waves = wave_number((ky + y_radix * inner).reshape(-1), y_total)
    lateral = x_waves[:, :, None] ** 2 + y_waves[None, None, :] ** 2
    kz_square = (omega * reference_slowness) ** 2 - lateral
    kz_root = jnp.sqrt(jnp.abs(kz_square))
    travels = kz_square >= 0.0
    amplitude = jnp.where(travels, 1.0, jnp.exp(-kz_root * depth_interval))
    amplitude = amplitude / (x_total * y_total)
    angles = jnp.where(travels, polarity * kz_root * depth_interval, 0.0)
    cosine, sine = cosine_sine(angles)
    return jnp.stack([amplitude * cosine, amplitude * sine], axis=1)


def zero_after(*others):
    corners = sum(other[(0,) * other.ndim] for other in others)
    return (corners * 0.0).astype(jnp.int32)


def per_device_fields(sizes, wavefields, slowness, freq_index):
    s, z, x, c = (lax.axis_index(axis) for axis in axes)
    rows, y_cols = wavefields.shape[3:]
    x_total = rows * sizes["gy"]
    place = jnp.stack([s, z, x, c]).astype(jnp.int32)

    def send(array, target):
        return lax.ppermute(array, axes, route(sizes, target))

    def to_core(array):
        return send(array, lambda s, z, x, c: (s, z, x, 1 - c))

    def to_partner(array):
        return send(array, lambda s, z, x, c: (s, z ^ 1, x, c))

    def to_partner_core(array):
        return send(array, lambda s, z, x, c: (s, z ^ 1, x, 1 - c))

    def to_freq(array):
        return send(array, lambda s, z, x, c: (s, z, 1 - x, c))

    def to_shot(array):
        return send(array, lambda s, z, x, c: (1 - s, z, x, c))

    def along_z(array, r):
        return send(array, lambda s, z, x, c: (s, z ^ r, x, c))

    row_forward = row_matrix(lanes, -1.0)
    row_inverse = row_matrix(lanes, 1.0)
    column_forward = column_matrix(rows // 2, -1.0)
    column_inverse = column_matrix(rows // 2, 1.0)

    width = y_cols // 8
    piece = lax.dynamic_slice_in_dim(slowness, (4 * s + 2 * x + c) * width, width, 2)
    pieces = [piece] + [along_z(piece, r) for r in (2, 3, 1)]

    def all_columns(late):
        stacked = jnp.stack([pieces[k] for k in (0, 3, 1, 2)], axis=1)
        mine = lax.dynamic_slice_in_dim(stacked, 2 * ((z // 2) ^ c) + late, 2, 1)
        theirs = to_core(
            lax.dynamic_slice_in_dim(stacked, 2 * ((z // 2) ^ (1 - c)) + late, 2, 1)
        )
        both = jnp.where(
            c == 0, jnp.concatenate([mine, theirs], 3), jnp.concatenate([theirs, mine], 3)
        )
        other = to_freq(both)
        pair = jnp.where(x == 0, jnp.stack([both, other]), jnp.stack([other, both]))
        far = to_shot(pair)
        return jnp.where(s == 0, jnp.concatenate([pair, far]), jnp.concatenate([far, pair]))

    y_steps = y_table(c, y_cols)
    spectra = origin_rows(wavefields[0], place, y_steps, row_forward)
    kept_is_odd = (z ^ c) % 2 == 1
    arrived = []
    for chunk in range(2):
        kept, crossed = spectra[chunk], to_core(spectra[2 + chunk])
        even = jnp.where(kept_is_odd, crossed, kept)
        odd = jnp.where(kept_is_odd, kept, crossed)
        far = along_z(even[1], 2)
        farthest = along_z(odd[1], 3)
        arrived.append([even[0], along_z(odd[0], 1), far, farthest])

    late = zero_after(arrived[0][1])
    layers = all_columns(late)

    z_late = z + late
    side = z_late % 2
    index = lax.dynamic_index_in_dim(freq_index, z_late // 2, 0, keepdims=False)
    omega = omega_unit * index.astype(jnp.float32)
    polarity = (2 * side - 1).astype(jnp.float32)
    order = 2 * c + side
    moves = [move_table(chunk, omega, polarity, c, x_total, y_cols) for chunk in range(2)]
    half = half_table(rows)
    table_z = x_table(z_late, x_total)
    table_order = x_table(order, x_total)
    scale = (polarity * omega).reshape(1)

    images = []
    blocks_in, order_in, table_in, hold = arrived, z, table_z, 0
    for depth_step in range(DEPTH):
        last = depth_step == DEPTH - 1
        swaps = jnp.stack([order_in & 1, order & 1]).astype(jnp.int32) + hold
        near, partner = [], []
        for chunk in range(2):
            out = move_columns(
                swaps, blocks_in[chunk], (table_in, table_order, half), moves[chunk],
                column_forward, column_inverse,
            )
            crossed = [to_core(out[2]), None if last else to_core(out[3])]
            near.append([[out[0], crossed[0]], [out[1], crossed[1]]])
            partner.append([to_partner(out[1]), to_partner_core(out[3])])

        def y_blocks(pairs):
            return [pairs[0][0], pairs[1][0], pairs[0][1], pairs[1][1]]

        own = y_blocks([near[0][0], near[1][0]])
        far_blocks = y_blocks(partner)
        if not last:
            turned = [None, None]
            waits = [zero_after(*partner[0]).astype(jnp.float32), 0.0]
            for slot in (1, 0):
                blocks = y_blocks([near[0][slot], near[1][slot]])
                turned[slot] = turn_rows(
                    slot == 0, (depth_step, slot), scale + waits[slot], blocks, layers, y_steps,
                    row_inverse, row_forward,
                )
            blocks_in = [
                [turned[0][k], turned[1][k], to_core(turned[0][2 + k]), to_core(turned[1][2 + k])]
                for k in range(2)
            ]
            hold = zero_after(*partner[1])
            order_in, table_in = order, table_order
            own = [turned[0][4]]
        terms = image_rows(
            (depth_step, 0), place, scale, own, far_blocks, layers, y_steps, row_inverse
        )

        def gather(r):
            def target(s, z, x, c):
                quarter = (2 * x + z // 2) ^ r
                return s, 2 * c + z % 2, quarter // 2, quarter % 2

            return send(terms[r], target)

        images.append(sum(gather(r) for r in range(4)))
    return jnp.stack(images)


def solution(mesh):
    sizes = dict(mesh.shape)

    def per_device(wavefields, slowness, freq_index):
        if fits_one_field_per_chip(sizes, wavefields.shape):
            return per_device_fields(sizes, wavefields, slowness, freq_index)
        return per_device_pencils(wavefields, slowness, freq_index)

    placed = (P("fld", None, ("shot", "freq"), "gy", None), P(None, "gy", None), P("freq"))
    return jax.shard_map(
        per_device,
        mesh=mesh,
        in_specs=placed,
        out_specs=P("shot", "gy", ("freq", "fld")),
        check_vma=False,
    )
```

```python
import functools
import math

import jax
import jax.numpy as jnp
import numpy as np
from jax import lax
from jax.experimental import pallas as pl
from jax.experimental.pallas import tpu as pltpu
from jax.sharding import PartitionSpec as P

DEPTH = 2


omega_unit = 0.1
reference_slowness = 1.0
depth_interval = 1.0
inner_length = 128


def contract(pattern, values, matrix):
    return jnp.einsum(
        pattern, values, matrix, precision=lax.Precision.HIGHEST, preferred_element_type=jnp.float32
    )


def complex_table(length, polarity):
    indices = jnp.arange(length, dtype=jnp.int32)
    angles = (
        2.0 * math.pi / length * (indices[:, None] * indices[None, :] % length).astype(jnp.float32)
    )
    cosine = jnp.cos(angles)
    sine_part = polarity * jnp.sin(angles)
    upper = jnp.stack([cosine, sine_part], axis=1)
    lower = jnp.stack([-sine_part, cosine], axis=1)
    return jnp.stack([upper, lower], axis=0)


def twiddle(outer_size, inner_size, length, polarity):
    outer_index = jnp.arange(outer_size, dtype=jnp.int32)[:, None]
    inner_index = jnp.arange(inner_size, dtype=jnp.int32)[None, :]
    angles = 2.0 * math.pi / length * (outer_index * inner_index % length).astype(jnp.float32)
    return (jnp.cos(angles), polarity * jnp.sin(angles))


def rotate(values, cosine, sine_part):
    real_part = values[0]
    imag_part = values[1]
    return jnp.stack(
        [real_part * cosine - imag_part * sine_part, real_part * sine_part + imag_part * cosine]
    )


def wave_number(indices, length):
    signed = jnp.where(indices < length // 2, indices, indices - length)
    return 2.0 * math.pi / length * signed.astype(jnp.float32)


def forward_rows(wave_field):
    batches, x_rows, y_cols = wave_field.shape[1:]
    outer_size = y_cols // inner_length
    blocks = wave_field.reshape(2, batches, x_rows, outer_size, inner_length)
    blocks = contract("cbxan,cadk->dbxkn", blocks, complex_table(outer_size, -1.0))
    cosine, sine_part = twiddle(outer_size, inner_length, y_cols, -1.0)
    blocks = rotate(blocks, cosine, sine_part)
    blocks = contract("cbxkn,cndm->dbxkm", blocks, complex_table(inner_length, -1.0))
    return blocks.reshape(2, batches, x_rows, y_cols)


def inverse_rows(wave_field):
    batches, x_rows, y_cols = wave_field.shape[1:]
    outer_size = y_cols // inner_length
    blocks = wave_field.reshape(2, batches, x_rows, outer_size, inner_length)
    blocks = contract("cbxkm,cmdn->dbxkn", blocks, complex_table(inner_length, 1.0))
    cosine, sine_part = twiddle(outer_size, inner_length, y_cols, 1.0)
    blocks = rotate(blocks, cosine, sine_part)
    blocks = contract("cbxkn,ckda->dbxan", blocks, complex_table(outer_size, 1.0))
    return blocks.reshape(2, batches, x_rows, y_cols) / y_cols


def forward_columns(blocks):
    inner_size = blocks.shape[2]
    pencils = blocks.shape[3]
    blocks = contract("cbnsy,csdk->dbnky", blocks, complex_table(pencils, -1.0))
    cosine, sine_part = twiddle(pencils, inner_size, inner_size * pencils, -1.0)
    blocks = rotate(blocks, cosine.T[:, :, None], sine_part.T[:, :, None])
    return contract("cbnky,cndm->dbmky", blocks, complex_table(inner_size, -1.0))


def inverse_columns(blocks):
    inner_size = blocks.shape[2]
    pencils = blocks.shape[3]
    blocks = contract("cbmky,cmdn->dbnky", blocks, complex_table(inner_size, 1.0))
    cosine, sine_part = twiddle(pencils, inner_size, inner_size * pencils, 1.0)
    blocks = rotate(blocks, cosine.T[:, :, None], sine_part.T[:, :, None])
    blocks = contract("cbnky,ckds->dbnsy", blocks, complex_table(pencils, 1.0))
    return blocks / (inner_size * pencils)


def propagate(blocks, omegas, polarities, y_total):
    inner_size, pencils, y_local = blocks.shape[2:]
    x_index = (
        jnp.arange(pencils, dtype=jnp.int32)[None, :]
        + pencils * jnp.arange(inner_size, dtype=jnp.int32)[:, None]
    )
    stored = lax.axis_index("gy") * y_local + jnp.arange(y_local, dtype=jnp.int32)
    y_index = stored // inner_length + y_total // inner_length * (stored % inner_length)
    x_waves = wave_number(x_index, inner_size * pencils)
    y_waves = wave_number(y_index, y_total)
    lateral = x_waves[:, :, None] ** 2 + y_waves[None, None, :] ** 2
    kz_square = ((omegas * reference_slowness) ** 2)[:, None, None, None] - lateral[None]
    kz_root = jnp.sqrt(jnp.abs(kz_square))
    travels = kz_square >= 0.0
    amplitude = jnp.where(travels, 1.0, jnp.exp(-kz_root * depth_interval))
    angles = jnp.where(travels, polarities[:, None, None, None] * kz_root * depth_interval, 0.0)
    return rotate(blocks, amplitude * jnp.cos(angles), amplitude * jnp.sin(angles))


def apply_screen(wave_field, slowness_now, omegas, polarities):
    phases = (polarities * omegas)[:, None, None] * (
        (slowness_now - reference_slowness) * depth_interval
    )[None]
    return rotate(wave_field, jnp.cos(phases), jnp.sin(phases))


def per_device_pencils(wavefields, slowness, freq_index):
    x_rows = wavefields.shape[3]
    y_cols = wavefields.shape[4]
    pencils = lax.axis_size("gy")
    freq_devs = lax.axis_size("freq")
    fld_devs = lax.axis_size("fld")
    column_width = y_cols // (freq_devs * fld_devs)
    omegas = omega_unit * freq_index.astype(jnp.float32)
    per_side = wavefields.shape[2] // fld_devs
    regrouped = wavefields.reshape(2, 1, fld_devs, per_side, x_rows, y_cols)
    paired = lax.all_to_all(regrouped, "fld", split_axis=2, concat_axis=1, tiled=True)
    wave_field = paired.reshape(2, fld_devs * per_side, x_rows, y_cols)
    local_omegas = lax.dynamic_slice_in_dim(omegas, lax.axis_index("fld") * per_side, per_side)
    omegas = jnp.tile(local_omegas, fld_devs)
    polarities = jnp.repeat(jnp.array([-1.0, 1.0], jnp.float32), per_side)
    batches = wave_field.shape[1]
    images = []
    for depth_step in range(DEPTH):
        wave_field = forward_rows(wave_field)
        blocks = wave_field.reshape(2, batches, x_rows, pencils, y_cols // pencils)
        blocks = lax.all_to_all(blocks, "gy", split_axis=3, concat_axis=3, tiled=True)
        blocks = forward_columns(blocks)
        blocks = propagate(blocks, omegas, polarities, y_cols)
        blocks = inverse_columns(blocks)
        blocks = lax.all_to_all(blocks, "gy", split_axis=3, concat_axis=3, tiled=True)
        wave_field = inverse_rows(blocks.reshape(2, batches, x_rows, y_cols))
        wave_field = apply_screen(wave_field, slowness[depth_step], omegas, polarities)
        source = wave_field[:, :per_side]
        receiver = wave_field[:, per_side:]
        summed = jnp.sum(source[0] * receiver[0] + source[1] * receiver[1], axis=0)
        partial_image = summed.reshape(x_rows, freq_devs * fld_devs, column_width)[None]
        images.append(
            lax.psum_scatter(partial_image, ("freq", "fld"), scatter_dimension=2, tiled=True)
        )
    combined = jnp.concatenate(images, axis=0)
    return combined.reshape(DEPTH, x_rows, column_width)


axes = ("shot", "gy", "freq", "fld")
lanes = 128
y_radix = 8
x_radix = 4
row_group = 32
strip = 16


def fits_one_field_per_chip(sizes, shape):
    return (
        sizes["gy"] == 4
        and sizes["freq"] == 2
        and sizes["fld"] == 2
        and shape[2] == 2
        and shape[4] == y_radix * lanes
        and shape[3] % row_group == 0
        and shape[3] * 4 == shape[4]
    )


def route(sizes, target):
    pairs = []
    for place in np.ndindex(*(sizes[axis] for axis in axes)):
        goal = target(*place)
        if goal is not None:
            dims = tuple(sizes[axis] for axis in axes)
            pairs.append(
                (int(np.ravel_multi_index(place, dims)), int(np.ravel_multi_index(goal, dims)))
            )
    return pairs


def split_constant(matrix):
    upper = matrix.astype(jnp.bfloat16)
    lower = (matrix - upper.astype(np.float64)).astype(jnp.bfloat16)
    return upper, lower


def dft_parts(length, polarity):
    indices = np.arange(length)
    angles = 2.0 * np.pi / length * (indices[:, None] * indices[None, :] % length)
    return np.cos(angles), polarity * np.sin(angles)


def row_matrix(length, polarity):
    cosine, sine = dft_parts(length, polarity)
    return split_constant(np.block([[cosine, sine], [-sine, cosine]]))


def column_matrix(length, polarity):
    cosine, sine = dft_parts(length, polarity)
    return split_constant(np.block([[cosine, -sine], [sine, cosine]]))


def add(one, two):
    return one[0] + two[0], one[1] + two[1]


def subtract(one, two):
    return one[0] - two[0], one[1] - two[1]


def multiply(one, two):
    return one[0] * two[0] - one[1] * two[1], one[0] * two[1] + one[1] * two[0]


def conjugate(one):
    return one[0], -one[1]


def quarter_turn(one, polarity):
    if polarity > 0:
        return -one[1], one[0]
    return one[1], -one[0]


def dft4(terms, polarity):
    even = add(terms[0], terms[2])
    odd = subtract(terms[0], terms[2])
    even_other = add(terms[1], terms[3])
    odd_other = quarter_turn(subtract(terms[1], terms[3]), polarity)
    return [
        add(even, even_other),
        add(odd, odd_other),
        subtract(even, even_other),
        subtract(odd, odd_other),
    ]


def eighth_turn(one, polarity):
    half = math.sqrt(0.5)
    if polarity > 0:
        return (one[0] - one[1]) * half, (one[0] + one[1]) * half
    return (one[0] + one[1]) * half, (one[1] - one[0]) * half


def dft8(terms, polarity):
    sums = [add(terms[a], terms[a + 4]) for a in range(4)]
    differences = [subtract(terms[a], terms[a + 4]) for a in range(4)]
    turned = [
        differences[0],
        eighth_turn(differences[1], polarity),
        quarter_turn(differences[2], polarity),
        quarter_turn(eighth_turn(differences[3], polarity), polarity),
    ]
    even = dft4(sums, polarity)
    odd = dft4(turned, polarity)
    return [even[k // 2] if k % 2 == 0 else odd[k // 2] for k in range(8)]


def two_parts(values):
    upper = values.astype(jnp.bfloat16)
    lower = (values - upper.astype(jnp.float32)).astype(jnp.bfloat16)
    return upper, lower


def dot(left, right):
    return jnp.dot(left, right, preferred_element_type=jnp.float32)


def rows_product(values, upper_ref, lower_ref):
    upper, lower = two_parts(values)
    return dot(upper, upper_ref[...]) + dot(lower, upper_ref[...]) + dot(upper, lower_ref[...])


def columns_product(upper_ref, lower_ref, upper, lower):
    return dot(upper_ref[...], upper) + dot(upper_ref[...], lower) + dot(lower_ref[...], upper)


def stack_blocks(terms):
    return jnp.concatenate([jnp.concatenate(term, axis=1) for term in terms], axis=0)


def unstack_blocks(values, rows):
    blocks = [values[k * rows : (k + 1) * rows] for k in range(y_radix)]
    return [(block[:, :lanes], block[:, lanes:]) for block in blocks]


def y_twiddle(table_ref, k):
    return table_ref[k, 0:1, :], table_ref[k, 1:2, :]


def forward_y(terms, table_ref, upper_ref, lower_ref):
    rows = terms[0][0].shape[0]
    turned = dft8(terms, -1.0)
    turned = [multiply(turned[k], y_twiddle(table_ref, k)) for k in range(y_radix)]
    return unstack_blocks(rows_product(stack_blocks(turned), upper_ref, lower_ref), rows)


def inverse_y(terms, table_ref, upper_ref, lower_ref):
    rows = terms[0][0].shape[0]
    inner = unstack_blocks(rows_product(stack_blocks(terms), upper_ref, lower_ref), rows)
    inner = [multiply(inner[k], conjugate(y_twiddle(table_ref, k))) for k in range(y_radix)]
    return dft8(inner, 1.0)


def lane_block(index):
    return slice(index * lanes, (index + 1) * lanes)


def row_groups(rows):
    return [slice(first, first + row_group) for first in range(0, rows, row_group)]


def origin_kernel(place_ref, field_ref, table_ref, upper_ref, lower_ref, *outs):
    sign = (1 - 2 * place_ref[3]).astype(jnp.float32)
    for rows in row_groups(field_ref.shape[2]):
        terms = []
        for a in range(y_radix):
            term = (field_ref[0, 0, rows, lane_block(a)], field_ref[1, 0, rows, lane_block(a)])
            terms.append((term[0] * sign, term[1] * sign) if a % 2 else term)
        spectrum = forward_y(terms, table_ref, upper_ref, lower_ref)
        for k in range(y_radix):
            for part in range(2):
                outs[k // 2][0, part, rows, lane_block(k % 2)] = spectrum[k][part]


def read_y_blocks(blocks, rows):
    return [
        tuple(blocks[k // 2][part, rows, lane_block(k % 2)] for part in range(2))
        for k in range(y_radix)
    ]


def read_layer(ref, at, rows):
    return [ref[a // 2, at[0], at[1], rows, lane_block(a % 2)] for a in range(y_radix)]


def screen_of(scale_ref, layer):
    phase = scale_ref[0] * ((layer - reference_slowness) * depth_interval)
    square = phase * phase
    cosine, sine = 1.0 / 40320.0, 1.0 / 362880.0
    for term in (-1.0 / 720.0, 1.0 / 24.0, -0.5, 1.0):
        cosine = cosine * square + term
    for term in (-1.0 / 5040.0, 1.0 / 120.0, -1.0 / 6.0, 1.0):
        sine = sine * square + term
    return cosine, sine * phase


def turn_kernel(keeps_field, at, scale_ref, *refs):
    blocks, layer_ref, refs = refs[:4], refs[4], refs[5:]
    table_ref, inv_upper, inv_lower, upper_ref, lower_ref = refs[:5]
    outs = refs[5:]
    for rows in row_groups(blocks[0].shape[1]):
        terms = inverse_y(read_y_blocks(blocks, rows), table_ref, inv_upper, inv_lower)
        layer = read_layer(layer_ref, at, rows)
        terms = [multiply(terms[a], screen_of(scale_ref, layer[a])) for a in range(y_radix)]
        if keeps_field:
            for a in range(y_radix):
                for part in range(2):
                    outs[4][part, rows, lane_block(a)] = terms[a][part]
        spectrum = forward_y(terms, table_ref, upper_ref, lower_ref)
        for k in range(y_radix):
            for part in range(2):
                outs[k // 2][part, rows, lane_block(k % 2)] = spectrum[k][part]


def image_kernel(own_ready, at, place_ref, scale_ref, *refs):
    own_count = 1 if own_ready else 4
    own, refs = refs[:own_count], refs[own_count:]
    blocks, layer_ref, refs = refs[:4], refs[4], refs[5:]
    table_ref, inv_upper, inv_lower = refs[:3]
    outs, quarters = refs[3:7], refs[7]
    for rows in row_groups(blocks[0].shape[1]):
        layer = read_layer(layer_ref, at, rows)
        other = inverse_y(read_y_blocks(blocks, rows), table_ref, inv_upper, inv_lower)
        if not own_ready:
            mine = inverse_y(read_y_blocks(own, rows), table_ref, inv_upper, inv_lower)
        for a in range(y_radix):
            screen = screen_of(scale_ref, layer[a])
            if own_ready:
                near = (own[0][0, rows, lane_block(a)], own[0][1, rows, lane_block(a)])
            else:
                near = multiply(mine[a], screen)
            far = multiply(other[a], conjugate(screen))
            quarters[a // 2, rows, lane_block(a % 2)] = near[0] * far[0] + near[1] * far[1]
    for r in range(4):
        outs[r][...] = quarters[lax.bitwise_xor(2 * place_ref[2] + place_ref[1] // 2, r)]


def x_kernel(swap_ref, *refs):
    blocks, refs = refs[:x_radix], refs[x_radix:]
    table_in, table_out, half_ref, move_ref, upper_ref, lower_ref, inv_upper, inv_lower = refs[:8]
    outs, (high, low, held) = refs[8:12], refs[12:]
    inner = blocks[0].shape[1] // 2

    def wide(table, *at):
        values = table[at]
        return jnp.concatenate([values] * (held.shape[2] // lanes), axis=1)

    def actual(k, swaps):
        return k if k % 2 == 0 else lax.bitwise_xor(k, 2 * swaps)

    def spans(step):
        first = pl.multiple_of(step * strip, strip)
        return pl.ds(first, strip), pl.ds(pl.multiple_of(first + inner, strip), strip)

    def gather_rows(step, carry):
        span, second = spans(step)
        halves = []
        for rows in (span, second):
            terms = dft4([(block[0, rows, :], block[1, rows, :]) for block in blocks], -1.0)
            halves.append(
                [
                    multiply(terms[k], (wide(table_in, k, 0, rows), wide(table_in, k, 1, rows)))
                    for k in range(x_radix)
                ]
            )
        turn = (wide(half_ref, 0, span), wide(half_ref, 1, span))
        for k in range(x_radix):
            goal = 2 * actual(k, swap_ref[0])
            pair = (
                add(halves[0][k], halves[1][k]),
                multiply(subtract(halves[0][k], halves[1][k]), turn),
            )
            for e in range(2):
                high[goal + e, span, :], low[goal + e, span, :] = two_parts(pair[e][0])
                high[goal + e, second, :], low[goal + e, second, :] = two_parts(pair[e][1])
        return carry

    lax.fori_loop(0, inner // strip, gather_rows, 0, unroll=2)

    for k in range(2 * x_radix):
        values = columns_product(upper_ref, lower_ref, high[k], low[k])
        moved = multiply((values[:inner], values[inner:]), (move_ref[k, 0], move_ref[k, 1]))
        upper, lower = two_parts(jnp.concatenate(moved, axis=0))
        held[k] = columns_product(inv_upper, inv_lower, upper, lower)

    def scatter_rows(step, carry):
        span, second = spans(step)
        turn = (wide(half_ref, 0, span), -wide(half_ref, 1, span))
        halves = [[], []]
        for k in range(x_radix):
            source = 2 * actual(k, swap_ref[1])
            even = (held[source, span, :], held[source, second, :])
            odd = multiply((held[source + 1, span, :], held[source + 1, second, :]), turn)
            for half, rows, term in ((0, span, add(even, odd)), (1, second, subtract(even, odd))):
                factor = (wide(table_out, k, 0, rows), -wide(table_out, k, 1, rows))
                halves[half].append(multiply(term, factor))
        for half, rows in ((0, span), (1, second)):
            terms = dft4(halves[half], 1.0)
            for q in range(x_radix):
                for part in range(2):
                    outs[q][part, rows, :] = terms[q][part]
        return carry

    lax.fori_loop(0, inner // strip, scatter_rows, 0, unroll=2)


smem = pl.BlockSpec(memory_space=pltpu.SMEM)
vmem = pl.BlockSpec(memory_space=pltpu.VMEM)
column_limit = 24 * 1024 * 1024
row_limit = 24 * 1024 * 1024


def estimate(microseconds):
    return pl.CostEstimate(
        flops=int(microseconds * 1e9), bytes_accessed=int(microseconds * 3e6), transcendentals=0
    )


def origin_rows(field, place, table, matrices):
    parts, freqs, rows, y_cols = field.shape
    width = y_cols // 4
    out = jax.ShapeDtypeStruct((freqs, parts, rows, width), jnp.float32)

    def fixed(array):
        return pl.BlockSpec(array.shape, lambda j, place: (0,) * array.ndim)

    return pl.pallas_call(
        origin_kernel,
        grid_spec=pltpu.PrefetchScalarGridSpec(
            num_scalar_prefetch=1,
            grid=(freqs,),
            in_specs=[
                pl.BlockSpec((parts, 1, rows, y_cols), lambda j, place: (0, j, 0, 0)),
                fixed(table),
                fixed(matrices[0]),
                fixed(matrices[1]),
            ],
            out_specs=[
                pl.BlockSpec(
                    (1, parts, rows, width),
                    lambda j, place: (lax.bitwise_xor(j, place[1] // 2), 0, 0, 0),
                )
            ]
            * 4,
        ),
        out_shape=[out] * 4,
        compiler_params=pltpu.CompilerParams(
            vmem_limit_bytes=32 * 1024 * 1024, dimension_semantics=("arbitrary",)
        ),
        cost_estimate=estimate(6),
        name="origin_rows",
    )(place, field, table, *matrices)


def turn_rows(keeps_field, at, scale, blocks, layers, table, inverse, forward):
    parts, rows, width = blocks[0].shape
    out = [jax.ShapeDtypeStruct((parts, rows, width), jnp.float32)] * 4
    if keeps_field:
        out = out + [jax.ShapeDtypeStruct((parts, rows, 4 * width), jnp.float32)]
    return pl.pallas_call(
        functools.partial(turn_kernel, keeps_field, at),
        in_specs=[smem] + [vmem] * 10,
        out_specs=[vmem] * len(out),
        out_shape=out,
        compiler_params=pltpu.CompilerParams(vmem_limit_bytes=row_limit),
        cost_estimate=estimate(4),
        name="turn_rows",
    )(scale, *blocks, layers, table, *inverse, *forward)


def image_rows(at, place, scale, own, blocks, layers, table, inverse):
    parts, rows, width = blocks[0].shape
    return pl.pallas_call(
        functools.partial(image_kernel, len(own) == 1, at),
        in_specs=[smem, smem] + [vmem] * (len(own) + 8),
        out_specs=[vmem] * 4,
        out_shape=[jax.ShapeDtypeStruct((rows, width), jnp.float32)] * 4,
        scratch_shapes=[pltpu.VMEM((4, rows, width), jnp.float32)],
        compiler_params=pltpu.CompilerParams(vmem_limit_bytes=row_limit),
        cost_estimate=estimate(3),
        name="image_rows",
    )(place, scale, *own, *blocks, layers, table, *inverse)


def move_columns(swaps, blocks, tables, move, forward, inverse):
    parts, rows, width = blocks[0].shape
    inner = parts * rows // 2
    return pl.pallas_call(
        x_kernel,
        in_specs=[smem] + [vmem] * (x_radix + 8),
        out_specs=[vmem] * x_radix,
        out_shape=[jax.ShapeDtypeStruct((parts, rows, width), jnp.float32)] * x_radix,
        scratch_shapes=[
            pltpu.VMEM((2 * x_radix, inner, width), jnp.bfloat16),
            pltpu.VMEM((2 * x_radix, inner, width), jnp.bfloat16),
            pltpu.VMEM((2 * x_radix, inner, width), jnp.float32),
        ],
        compiler_params=pltpu.CompilerParams(vmem_limit_bytes=column_limit),
        cost_estimate=estimate(6),
        name="move_columns",
    )(swaps, *blocks, *tables, move, *forward, *inverse)


def y_table(core, y_cols):
    k = (jnp.arange(y_radix, dtype=jnp.int32) ^ (4 * core))[:, None]
    r = jnp.arange(lanes, dtype=jnp.int32)[None, :]
    angles = 2.0 * math.pi / y_cols * (k * r % y_cols).astype(jnp.float32)
    return jnp.stack([jnp.cos(angles), -jnp.sin(angles)], axis=1)


def x_table(order, x_total):
    rows = x_total // x_radix
    low_bit, high_bit = order & 1, order >> 1
    slot = jnp.arange(x_radix, dtype=jnp.int32)
    k = jnp.where(slot % 2 == 1, slot ^ (2 * low_bit), slot)
    eighths = jnp.where(k % 2 == 1, 4 * high_bit, 0)
    turns = jnp.array([0, 6, 4, 2], jnp.int32)
    eighths = eighths + low_bit * turns[k]
    row = jnp.arange(rows, dtype=jnp.int32)[None, :]
    steps = (x_total // 8 * eighths[:, None] - k[:, None] * row) % x_total
    angles = 2.0 * math.pi / x_total * steps.astype(jnp.float32)
    table = jnp.stack([jnp.cos(angles), jnp.sin(angles)], axis=1)
    return jnp.broadcast_to(table[..., None], table.shape + (lanes,))


def cosine_sine(angles):
    half = 0.5 * angles
    square = half * half
    cosine, sine = 1.0 / math.factorial(12), -1.0 / math.factorial(11)
    for order in (10, 8, 6, 4, 2, 0):
        sign = -1.0 if order % 4 else 1.0
        cosine = cosine * square + sign / math.factorial(order)
        if order:
            sine = sine * square - sign / math.factorial(order - 1)
    sine = sine * half
    return 1.0 - 2.0 * sine * sine, 2.0 * sine * cosine


def half_table(rows):
    angles = -2.0 * np.pi / rows * np.arange(rows // 2)
    table = np.stack([np.cos(angles), np.sin(angles)]).astype(np.float32)
    return jnp.asarray(np.ascontiguousarray(np.broadcast_to(table[..., None], table.shape + (lanes,))))


def move_table(chunk, omega, polarity, core, x_total, y_total):
    step = jnp.arange(2 * x_radix, dtype=jnp.int32)[:, None]
    inner = jnp.arange(x_total // (2 * x_radix), dtype=jnp.int32)[None, :]
    x_waves = wave_number(step // 2 + x_radix * (2 * inner + step % 2), x_total)
    ky = jnp.arange(2, dtype=jnp.int32)[:, None] + 2 * chunk + y_radix // 2 * core
    inner = jnp.arange(lanes, dtype=jnp.int32)[None, :]
    y_waves = wave_number((ky + y_radix * inner).reshape(-1), y_total)
    lateral = x_waves[:, :, None] ** 2 + y_waves[None, None, :] ** 2
    kz_square = (omega * reference_slowness) ** 2 - lateral
    kz_root = jnp.sqrt(jnp.abs(kz_square))
    travels = kz_square >= 0.0
    amplitude = jnp.where(travels, 1.0, jnp.exp(-kz_root * depth_interval))
    amplitude = amplitude / (x_total * y_total)
    angles = jnp.where(travels, polarity * kz_root * depth_interval, 0.0)
    cosine, sine = cosine_sine(angles)
    return jnp.stack([amplitude * cosine, amplitude * sine], axis=1)


def zero_after(*others):
    corners = sum(other[(0,) * other.ndim] for other in others)
    return (corners * 0.0).astype(jnp.int32)


def per_device_fields(sizes, wavefields, slowness, freq_index):
    s, z, x, c = (lax.axis_index(axis) for axis in axes)
    rows, y_cols = wavefields.shape[3:]
    x_total = rows * sizes["gy"]
    place = jnp.stack([s, z, x, c]).astype(jnp.int32)

    def send(array, target):
        return lax.ppermute(array, axes, route(sizes, target))

    def to_core(array):
        return send(array, lambda s, z, x, c: (s, z, x, 1 - c))

    def to_partner(array):
        return send(array, lambda s, z, x, c: (s, z ^ 1, x, c))

    def to_partner_core(array):
        return send(array, lambda s, z, x, c: (s, z ^ 1, x, 1 - c))

    def to_freq(array):
        return send(array, lambda s, z, x, c: (s, z, 1 - x, c))

    def to_shot(array):
        return send(array, lambda s, z, x, c: (1 - s, z, x, c))

    def along_z(array, r):
        return send(array, lambda s, z, x, c: (s, z ^ r, x, c))

    row_forward = row_matrix(lanes, -1.0)
    row_inverse = row_matrix(lanes, 1.0)
    column_forward = column_matrix(rows // 2, -1.0)
    column_inverse = column_matrix(rows // 2, 1.0)

    width = y_cols // 8
    piece = lax.dynamic_slice_in_dim(slowness, (4 * s + 2 * x + c) * width, width, 2)
    pieces = [piece] + [along_z(piece, r) for r in (2, 3, 1)]

    def all_columns(late):
        stacked = jnp.stack([pieces[k] for k in (0, 3, 1, 2)], axis=1)
        mine = lax.dynamic_slice_in_dim(stacked, 2 * ((z // 2) ^ c) + late, 2, 1)
        theirs = to_core(
            lax.dynamic_slice_in_dim(stacked, 2 * ((z // 2) ^ (1 - c)) + late, 2, 1)
        )
        both = jnp.where(
            c == 0, jnp.concatenate([mine, theirs], 3), jnp.concatenate([theirs, mine], 3)
        )
        other = to_freq(both)
        pair = jnp.where(x == 0, jnp.stack([both, other]), jnp.stack([other, both]))
        far = to_shot(pair)
        return jnp.where(s == 0, jnp.concatenate([pair, far]), jnp.concatenate([far, pair]))

    y_steps = y_table(c, y_cols)
    spectra = origin_rows(wavefields[0], place, y_steps, row_forward)
    kept_is_odd = (z ^ c) % 2 == 1
    arrived = []
    for chunk in range(2):
        kept, crossed = spectra[chunk], to_core(spectra[2 + chunk])
        even = jnp.where(kept_is_odd, crossed, kept)
        odd = jnp.where(kept_is_odd, kept, crossed)
        far = along_z(even[1], 2)
        farthest = along_z(odd[1], 3)
        arrived.append([even[0], along_z(odd[0], 1), far, farthest])

    late = zero_after(arrived[0][1])
    layers = all_columns(late)

    z_late = z + late
    side = z_late % 2
    index = lax.dynamic_index_in_dim(freq_index, z_late // 2, 0, keepdims=False)
    omega = omega_unit * index.astype(jnp.float32)
    polarity = (2 * side - 1).astype(jnp.float32)
    order = 2 * c + side
    moves = [move_table(chunk, omega, polarity, c, x_total, y_cols) for chunk in range(2)]
    half = half_table(rows)
    table_z = x_table(z_late, x_total)
    table_order = x_table(order, x_total)
    scale = (polarity * omega).reshape(1)

    images = []
    blocks_in, order_in, table_in, hold = arrived, z, table_z, 0
    for depth_step in range(DEPTH):
        last = depth_step == DEPTH - 1
        swaps = jnp.stack([order_in & 1, order & 1]).astype(jnp.int32) + hold
        near, partner = [], []
        for chunk in range(2):
            out = move_columns(
                swaps, blocks_in[chunk], (table_in, table_order, half), moves[chunk],
                column_forward, column_inverse,
            )
            crossed = [to_core(out[2]), None if last else to_core(out[3])]
            near.append([[out[0], crossed[0]], [out[1], crossed[1]]])
            partner.append([to_partner(out[1]), to_partner_core(out[3])])

        def y_blocks(pairs):
            return [pairs[0][0], pairs[1][0], pairs[0][1], pairs[1][1]]

        own = y_blocks([near[0][0], near[1][0]])
        far_blocks = y_blocks(partner)
        if not last:
            turned = [None, None]
            waits = [zero_after(*partner[0]).astype(jnp.float32), 0.0]
            for slot in (1, 0):
                blocks = y_blocks([near[0][slot], near[1][slot]])
                turned[slot] = turn_rows(
                    slot == 0, (depth_step, slot), scale + waits[slot], blocks, layers, y_steps,
                    row_inverse, row_forward,
                )
            blocks_in = [
                [turned[0][k], turned[1][k], to_core(turned[0][2 + k]), to_core(turned[1][2 + k])]
                for k in range(2)
            ]
            hold = zero_after(partner[1][0])
            order_in, table_in = order, table_order
            own = [turned[0][4]]
        terms = image_rows(
            (depth_step, 0), place, scale, own, far_blocks, layers, y_steps, row_inverse
        )

        def gather(r):
            def target(s, z, x, c):
                quarter = (2 * x + z // 2) ^ r
                return s, 2 * c + z % 2, quarter // 2, quarter % 2

            return send(terms[r], target)

        images.append(sum(gather(r) for r in range(4)))
    return jnp.stack(images)


def solution(mesh):
    sizes = dict(mesh.shape)

    def per_device(wavefields, slowness, freq_index):
        if fits_one_field_per_chip(sizes, wavefields.shape):
            return per_device_fields(sizes, wavefields, slowness, freq_index)
        return per_device_pencils(wavefields, slowness, freq_index)

    placed = (P("fld", None, ("shot", "freq"), "gy", None), P(None, "gy", None), P("freq"))
    return jax.shard_map(
        per_device,
        mesh=mesh,
        in_specs=placed,
        out_specs=P("shot", "gy", ("freq", "fld")),
        check_vma=False,
    )
```

```python
import functools
import math

import jax
import jax.numpy as jnp
import numpy as np
from jax import lax
from jax.experimental import pallas as pl
from jax.experimental.pallas import tpu as pltpu
from jax.sharding import PartitionSpec as P

DEPTH = 2


omega_unit = 0.1
reference_slowness = 1.0
depth_interval = 1.0
inner_length = 128


def contract(pattern, values, matrix):
    return jnp.einsum(
        pattern, values, matrix, precision=lax.Precision.HIGHEST, preferred_element_type=jnp.float32
    )


def complex_table(length, polarity):
    indices = jnp.arange(length, dtype=jnp.int32)
    angles = (
        2.0 * math.pi / length * (indices[:, None] * indices[None, :] % length).astype(jnp.float32)
    )
    cosine = jnp.cos(angles)
    sine_part = polarity * jnp.sin(angles)
    upper = jnp.stack([cosine, sine_part], axis=1)
    lower = jnp.stack([-sine_part, cosine], axis=1)
    return jnp.stack([upper, lower], axis=0)


def twiddle(outer_size, inner_size, length, polarity):
    outer_index = jnp.arange(outer_size, dtype=jnp.int32)[:, None]
    inner_index = jnp.arange(inner_size, dtype=jnp.int32)[None, :]
    angles = 2.0 * math.pi / length * (outer_index * inner_index % length).astype(jnp.float32)
    return (jnp.cos(angles), polarity * jnp.sin(angles))


def rotate(values, cosine, sine_part):
    real_part = values[0]
    imag_part = values[1]
    return jnp.stack(
        [real_part * cosine - imag_part * sine_part, real_part * sine_part + imag_part * cosine]
    )


def wave_number(indices, length):
    signed = jnp.where(indices < length // 2, indices, indices - length)
    return 2.0 * math.pi / length * signed.astype(jnp.float32)


def forward_rows(wave_field):
    batches, x_rows, y_cols = wave_field.shape[1:]
    outer_size = y_cols // inner_length
    blocks = wave_field.reshape(2, batches, x_rows, outer_size, inner_length)
    blocks = contract("cbxan,cadk->dbxkn", blocks, complex_table(outer_size, -1.0))
    cosine, sine_part = twiddle(outer_size, inner_length, y_cols, -1.0)
    blocks = rotate(blocks, cosine, sine_part)
    blocks = contract("cbxkn,cndm->dbxkm", blocks, complex_table(inner_length, -1.0))
    return blocks.reshape(2, batches, x_rows, y_cols)


def inverse_rows(wave_field):
    batches, x_rows, y_cols = wave_field.shape[1:]
    outer_size = y_cols // inner_length
    blocks = wave_field.reshape(2, batches, x_rows, outer_size, inner_length)
    blocks = contract("cbxkm,cmdn->dbxkn", blocks, complex_table(inner_length, 1.0))
    cosine, sine_part = twiddle(outer_size, inner_length, y_cols, 1.0)
    blocks = rotate(blocks, cosine, sine_part)
    blocks = contract("cbxkn,ckda->dbxan", blocks, complex_table(outer_size, 1.0))
    return blocks.reshape(2, batches, x_rows, y_cols) / y_cols


def forward_columns(blocks):
    inner_size = blocks.shape[2]
    pencils = blocks.shape[3]
    blocks = contract("cbnsy,csdk->dbnky", blocks, complex_table(pencils, -1.0))
    cosine, sine_part = twiddle(pencils, inner_size, inner_size * pencils, -1.0)
    blocks = rotate(blocks, cosine.T[:, :, None], sine_part.T[:, :, None])
    return contract("cbnky,cndm->dbmky", blocks, complex_table(inner_size, -1.0))


def inverse_columns(blocks):
    inner_size = blocks.shape[2]
    pencils = blocks.shape[3]
    blocks = contract("cbmky,cmdn->dbnky", blocks, complex_table(inner_size, 1.0))
    cosine, sine_part = twiddle(pencils, inner_size, inner_size * pencils, 1.0)
    blocks = rotate(blocks, cosine.T[:, :, None], sine_part.T[:, :, None])
    blocks = contract("cbnky,ckds->dbnsy", blocks, complex_table(pencils, 1.0))
    return blocks / (inner_size * pencils)


def propagate(blocks, omegas, polarities, y_total):
    inner_size, pencils, y_local = blocks.shape[2:]
    x_index = (
        jnp.arange(pencils, dtype=jnp.int32)[None, :]
        + pencils * jnp.arange(inner_size, dtype=jnp.int32)[:, None]
    )
    stored = lax.axis_index("gy") * y_local + jnp.arange(y_local, dtype=jnp.int32)
    y_index = stored // inner_length + y_total // inner_length * (stored % inner_length)
    x_waves = wave_number(x_index, inner_size * pencils)
    y_waves = wave_number(y_index, y_total)
    lateral = x_waves[:, :, None] ** 2 + y_waves[None, None, :] ** 2
    kz_square = ((omegas * reference_slowness) ** 2)[:, None, None, None] - lateral[None]
    kz_root = jnp.sqrt(jnp.abs(kz_square))
    travels = kz_square >= 0.0
    amplitude = jnp.where(travels, 1.0, jnp.exp(-kz_root * depth_interval))
    angles = jnp.where(travels, polarities[:, None, None, None] * kz_root * depth_interval, 0.0)
    return rotate(blocks, amplitude * jnp.cos(angles), amplitude * jnp.sin(angles))


def apply_screen(wave_field, slowness_now, omegas, polarities):
    phases = (polarities * omegas)[:, None, None] * (
        (slowness_now - reference_slowness) * depth_interval
    )[None]
    return rotate(wave_field, jnp.cos(phases), jnp.sin(phases))


def per_device_pencils(wavefields, slowness, freq_index):
    x_rows = wavefields.shape[3]
    y_cols = wavefields.shape[4]
    pencils = lax.axis_size("gy")
    freq_devs = lax.axis_size("freq")
    fld_devs = lax.axis_size("fld")
    column_width = y_cols // (freq_devs * fld_devs)
    omegas = omega_unit * freq_index.astype(jnp.float32)
    per_side = wavefields.shape[2] // fld_devs
    regrouped = wavefields.reshape(2, 1, fld_devs, per_side, x_rows, y_cols)
    paired = lax.all_to_all(regrouped, "fld", split_axis=2, concat_axis=1, tiled=True)
    wave_field = paired.reshape(2, fld_devs * per_side, x_rows, y_cols)
    local_omegas = lax.dynamic_slice_in_dim(omegas, lax.axis_index("fld") * per_side, per_side)
    omegas = jnp.tile(local_omegas, fld_devs)
    polarities = jnp.repeat(jnp.array([-1.0, 1.0], jnp.float32), per_side)
    batches = wave_field.shape[1]
    images = []
    for depth_step in range(DEPTH):
        wave_field = forward_rows(wave_field)
        blocks = wave_field.reshape(2, batches, x_rows, pencils, y_cols // pencils)
        blocks = lax.all_to_all(blocks, "gy", split_axis=3, concat_axis=3, tiled=True)
        blocks = forward_columns(blocks)
        blocks = propagate(blocks, omegas, polarities, y_cols)
        blocks = inverse_columns(blocks)
        blocks = lax.all_to_all(blocks, "gy", split_axis=3, concat_axis=3, tiled=True)
        wave_field = inverse_rows(blocks.reshape(2, batches, x_rows, y_cols))
        wave_field = apply_screen(wave_field, slowness[depth_step], omegas, polarities)
        source = wave_field[:, :per_side]
        receiver = wave_field[:, per_side:]
        summed = jnp.sum(source[0] * receiver[0] + source[1] * receiver[1], axis=0)
        partial_image = summed.reshape(x_rows, freq_devs * fld_devs, column_width)[None]
        images.append(
            lax.psum_scatter(partial_image, ("freq", "fld"), scatter_dimension=2, tiled=True)
        )
    combined = jnp.concatenate(images, axis=0)
    return combined.reshape(DEPTH, x_rows, column_width)


axes = ("shot", "gy", "freq", "fld")
lanes = 128
y_radix = 8
x_radix = 4
row_group = 32
strip = 16


def fits_one_field_per_chip(sizes, shape):
    return (
        sizes["gy"] == 4
        and sizes["freq"] == 2
        and sizes["fld"] == 2
        and shape[2] == 2
        and shape[4] == y_radix * lanes
        and shape[3] % row_group == 0
        and shape[3] * 4 == shape[4]
    )


def route(sizes, target):
    pairs = []
    for place in np.ndindex(*(sizes[axis] for axis in axes)):
        goal = target(*place)
        if goal is not None:
            dims = tuple(sizes[axis] for axis in axes)
            pairs.append(
                (int(np.ravel_multi_index(place, dims)), int(np.ravel_multi_index(goal, dims)))
            )
    return pairs


def split_constant(matrix):
    upper = matrix.astype(jnp.bfloat16)
    lower = (matrix - upper.astype(np.float64)).astype(jnp.bfloat16)
    return upper, lower


def dft_parts(length, polarity):
    indices = np.arange(length)
    angles = 2.0 * np.pi / length * (indices[:, None] * indices[None, :] % length)
    return np.cos(angles), polarity * np.sin(angles)


def row_matrix(length, polarity):
    cosine, sine = dft_parts(length, polarity)
    return split_constant(np.block([[cosine, sine], [-sine, cosine]]))


def column_matrix(length, polarity):
    cosine, sine = dft_parts(length, polarity)
    return split_constant(np.block([[cosine, -sine], [sine, cosine]]))


def add(one, two):
    return one[0] + two[0], one[1] + two[1]


def subtract(one, two):
    return one[0] - two[0], one[1] - two[1]


def multiply(one, two):
    return one[0] * two[0] - one[1] * two[1], one[0] * two[1] + one[1] * two[0]


def conjugate(one):
    return one[0], -one[1]


def quarter_turn(one, polarity):
    if polarity > 0:
        return -one[1], one[0]
    return one[1], -one[0]


def dft4(terms, polarity):
    even = add(terms[0], terms[2])
    odd = subtract(terms[0], terms[2])
    even_other = add(terms[1], terms[3])
    odd_other = quarter_turn(subtract(terms[1], terms[3]), polarity)
    return [
        add(even, even_other),
        add(odd, odd_other),
        subtract(even, even_other),
        subtract(odd, odd_other),
    ]


def eighth_turn(one, polarity):
    half = math.sqrt(0.5)
    if polarity > 0:
        return (one[0] - one[1]) * half, (one[0] + one[1]) * half
    return (one[0] + one[1]) * half, (one[1] - one[0]) * half


def dft8(terms, polarity):
    sums = [add(terms[a], terms[a + 4]) for a in range(4)]
    differences = [subtract(terms[a], terms[a + 4]) for a in range(4)]
    turned = [
        differences[0],
        eighth_turn(differences[1], polarity),
        quarter_turn(differences[2], polarity),
        quarter_turn(eighth_turn(differences[3], polarity), polarity),
    ]
    even = dft4(sums, polarity)
    odd = dft4(turned, polarity)
    return [even[k // 2] if k % 2 == 0 else odd[k // 2] for k in range(8)]


def two_parts(values):
    upper = values.astype(jnp.bfloat16)
    lower = (values - upper.astype(jnp.float32)).astype(jnp.bfloat16)
    return upper, lower


def dot(left, right):
    return jnp.dot(left, right, preferred_element_type=jnp.float32)


def rows_product(values, upper_ref, lower_ref):
    upper, lower = two_parts(values)
    return dot(upper, upper_ref[...]) + dot(lower, upper_ref[...]) + dot(upper, lower_ref[...])


def columns_product(upper_ref, lower_ref, upper, lower):
    return dot(upper_ref[...], upper) + dot(upper_ref[...], lower) + dot(lower_ref[...], upper)


def stack_blocks(terms):
    return jnp.concatenate([jnp.concatenate(term, axis=1) for term in terms], axis=0)


def unstack_blocks(values, rows):
    blocks = [values[k * rows : (k + 1) * rows] for k in range(y_radix)]
    return [(block[:, :lanes], block[:, lanes:]) for block in blocks]


def y_twiddle(table_ref, k):
    return table_ref[k, 0:1, :], table_ref[k, 1:2, :]


def forward_y(terms, table_ref, upper_ref, lower_ref):
    rows = terms[0][0].shape[0]
    turned = dft8(terms, -1.0)
    turned = [multiply(turned[k], y_twiddle(table_ref, k)) for k in range(y_radix)]
    return unstack_blocks(rows_product(stack_blocks(turned), upper_ref, lower_ref), rows)


def inverse_y(terms, table_ref, upper_ref, lower_ref):
    rows = terms[0][0].shape[0]
    inner = unstack_blocks(rows_product(stack_blocks(terms), upper_ref, lower_ref), rows)
    inner = [multiply(inner[k], conjugate(y_twiddle(table_ref, k))) for k in range(y_radix)]
    return dft8(inner, 1.0)


def lane_block(index):
    return slice(index * lanes, (index + 1) * lanes)


def row_groups(rows):
    return [slice(first, first + row_group) for first in range(0, rows, row_group)]


def origin_kernel(place_ref, field_ref, table_ref, upper_ref, lower_ref, *outs):
    sign = (1 - 2 * place_ref[3]).astype(jnp.float32)
    for rows in row_groups(field_ref.shape[2]):
        terms = []
        for a in range(y_radix):
            term = (field_ref[0, 0, rows, lane_block(a)], field_ref[1, 0, rows, lane_block(a)])
            terms.append((term[0] * sign, term[1] * sign) if a % 2 else term)
        spectrum = forward_y(terms, table_ref, upper_ref, lower_ref)
        for k in range(y_radix):
            for part in range(2):
                outs[k // 2][0, part, rows, lane_block(k % 2)] = spectrum[k][part]


def read_y_blocks(blocks, rows):
    return [
        tuple(blocks[k // 2][part, rows, lane_block(k % 2)] for part in range(2))
        for k in range(y_radix)
    ]


def read_layer(place_ref, near_ref, far_ref, at, rows):
    layer = []
    for a in range(y_radix):
        g = a // 2
        index = (g % 2, at[0], at[1], rows, lane_block(a % 2))
        layer.append(jnp.where(place_ref[0] == g // 2, near_ref[index], far_ref[index]))
    return layer


def screen_of(scale_ref, layer):
    phase = scale_ref[0] * ((layer - reference_slowness) * depth_interval)
    square = phase * phase
    cosine, sine = 1.0 / 40320.0, 1.0 / 362880.0
    for term in (-1.0 / 720.0, 1.0 / 24.0, -0.5, 1.0):
        cosine = cosine * square + term
    for term in (-1.0 / 5040.0, 1.0 / 120.0, -1.0 / 6.0, 1.0):
        sine = sine * square + term
    return cosine, sine * phase


def turn_kernel(keeps_field, at, place_ref, scale_ref, *refs):
    blocks, layer_refs, refs = refs[:4], refs[4:6], refs[6:]
    table_ref, inv_upper, inv_lower, upper_ref, lower_ref = refs[:5]
    outs = refs[5:]
    for rows in row_groups(blocks[0].shape[1]):
        terms = inverse_y(read_y_blocks(blocks, rows), table_ref, inv_upper, inv_lower)
        layer = read_layer(place_ref, *layer_refs, at, rows)
        terms = [multiply(terms[a], screen_of(scale_ref, layer[a])) for a in range(y_radix)]
        if keeps_field:
            for a in range(y_radix):
                for part in range(2):
                    outs[4][part, rows, lane_block(a)] = terms[a][part]
        spectrum = forward_y(terms, table_ref, upper_ref, lower_ref)
        for k in range(y_radix):
            for part in range(2):
                outs[k // 2][part, rows, lane_block(k % 2)] = spectrum[k][part]


def image_kernel(own_ready, at, place_ref, scale_ref, *refs):
    own_count = 1 if own_ready else 4
    own, refs = refs[:own_count], refs[own_count:]
    blocks, layer_refs, refs = refs[:4], refs[4:6], refs[6:]
    table_ref, inv_upper, inv_lower = refs[:3]
    outs, quarters = refs[3:7], refs[7]
    for rows in row_groups(blocks[0].shape[1]):
        layer = read_layer(place_ref, *layer_refs, at, rows)
        other = inverse_y(read_y_blocks(blocks, rows), table_ref, inv_upper, inv_lower)
        if not own_ready:
            mine = inverse_y(read_y_blocks(own, rows), table_ref, inv_upper, inv_lower)
        for a in range(y_radix):
            screen = screen_of(scale_ref, layer[a])
            if own_ready:
                near = (own[0][0, rows, lane_block(a)], own[0][1, rows, lane_block(a)])
            else:
                near = multiply(mine[a], screen)
            far = multiply(other[a], conjugate(screen))
            quarters[a // 2, rows, lane_block(a % 2)] = near[0] * far[0] + near[1] * far[1]
    for r in range(4):
        outs[r][...] = quarters[lax.bitwise_xor(2 * place_ref[2] + place_ref[1] // 2, r)]


def x_kernel(swap_ref, *refs):
    blocks, refs = refs[:x_radix], refs[x_radix:]
    table_in, table_out, half_ref, move_ref, upper_ref, lower_ref, inv_upper, inv_lower = refs[:8]
    outs, (high, low, held) = refs[8:12], refs[12:]
    inner = blocks[0].shape[1] // 2

    def wide(table, *at):
        values = table[at]
        return jnp.concatenate([values] * (held.shape[2] // lanes), axis=1)

    def actual(k, swaps):
        return k if k % 2 == 0 else lax.bitwise_xor(k, 2 * swaps)

    def spans(step):
        first = pl.multiple_of(step * strip, strip)
        return pl.ds(first, strip), pl.ds(pl.multiple_of(first + inner, strip), strip)

    def gather_rows(step, carry):
        span, second = spans(step)
        halves = []
        for rows in (span, second):
            terms = dft4([(block[0, rows, :], block[1, rows, :]) for block in blocks], -1.0)
            halves.append(
                [
                    multiply(terms[k], (wide(table_in, k, 0, rows), wide(table_in, k, 1, rows)))
                    for k in range(x_radix)
                ]
            )
        turn = (wide(half_ref, 0, span), wide(half_ref, 1, span))
        for k in range(x_radix):
            goal = 2 * actual(k, swap_ref[0])
            pair = (
                add(halves[0][k], halves[1][k]),
                multiply(subtract(halves[0][k], halves[1][k]), turn),
            )
            for e in range(2):
                high[goal + e, span, :], low[goal + e, span, :] = two_parts(pair[e][0])
                high[goal + e, second, :], low[goal + e, second, :] = two_parts(pair[e][1])
        return carry

    lax.fori_loop(0, inner // strip, gather_rows, 0, unroll=2)

    for k in range(2 * x_radix):
        values = columns_product(upper_ref, lower_ref, high[k], low[k])
        moved = multiply((values[:inner], values[inner:]), (move_ref[k, 0], move_ref[k, 1]))
        upper, lower = two_parts(jnp.concatenate(moved, axis=0))
        held[k] = columns_product(inv_upper, inv_lower, upper, lower)

    def scatter_rows(step, carry):
        span, second = spans(step)
        turn = (wide(half_ref, 0, span), -wide(half_ref, 1, span))
        halves = [[], []]
        for k in range(x_radix):
            source = 2 * actual(k, swap_ref[1])
            even = (held[source, span, :], held[source, second, :])
            odd = multiply((held[source + 1, span, :], held[source + 1, second, :]), turn)
            for half, rows, term in ((0, span, add(even, odd)), (1, second, subtract(even, odd))):
                factor = (wide(table_out, k, 0, rows), -wide(table_out, k, 1, rows))
                halves[half].append(multiply(term, factor))
        for half, rows in ((0, span), (1, second)):
            terms = dft4(halves[half], 1.0)
            for q in range(x_radix):
                for part in range(2):
                    outs[q][part, rows, :] = terms[q][part]
        return carry

    lax.fori_loop(0, inner // strip, scatter_rows, 0, unroll=2)


smem = pl.BlockSpec(memory_space=pltpu.SMEM)
vmem = pl.BlockSpec(memory_space=pltpu.VMEM)
column_limit = 24 * 1024 * 1024
row_limit = 24 * 1024 * 1024


def estimate(microseconds):
    return pl.CostEstimate(
        flops=int(microseconds * 1e9), bytes_accessed=int(microseconds * 3e6), transcendentals=0
    )


def origin_rows(field, place, table, matrices):
    parts, freqs, rows, y_cols = field.shape
    width = y_cols // 4
    out = jax.ShapeDtypeStruct((freqs, parts, rows, width), jnp.float32)

    def fixed(array):
        return pl.BlockSpec(array.shape, lambda j, place: (0,) * array.ndim)

    return pl.pallas_call(
        origin_kernel,
        grid_spec=pltpu.PrefetchScalarGridSpec(
            num_scalar_prefetch=1,
            grid=(freqs,),
            in_specs=[
                pl.BlockSpec((parts, 1, rows, y_cols), lambda j, place: (0, j, 0, 0)),
                fixed(table),
                fixed(matrices[0]),
                fixed(matrices[1]),
            ],
            out_specs=[
                pl.BlockSpec(
                    (1, parts, rows, width),
                    lambda j, place: (lax.bitwise_xor(j, place[1] // 2), 0, 0, 0),
                )
            ]
            * 4,
        ),
        out_shape=[out] * 4,
        compiler_params=pltpu.CompilerParams(
            vmem_limit_bytes=32 * 1024 * 1024, dimension_semantics=("arbitrary",)
        ),
        cost_estimate=estimate(6),
        name="origin_rows",
    )(place, field, table, *matrices)


def turn_rows(keeps_field, at, place, scale, blocks, layers, table, inverse, forward):
    parts, rows, width = blocks[0].shape
    out = [jax.ShapeDtypeStruct((parts, rows, width), jnp.float32)] * 4
    if keeps_field:
        out = out + [jax.ShapeDtypeStruct((parts, rows, 4 * width), jnp.float32)]
    return pl.pallas_call(
        functools.partial(turn_kernel, keeps_field, at),
        in_specs=[smem, smem] + [vmem] * 11,
        out_specs=[vmem] * len(out),
        out_shape=out,
        compiler_params=pltpu.CompilerParams(vmem_limit_bytes=row_limit),
        cost_estimate=estimate(4),
        name="turn_rows",
    )(place, scale, *blocks, *layers, table, *inverse, *forward)


def image_rows(at, place, scale, own, blocks, layers, table, inverse):
    parts, rows, width = blocks[0].shape
    return pl.pallas_call(
        functools.partial(image_kernel, len(own) == 1, at),
        in_specs=[smem, smem] + [vmem] * (len(own) + 9),
        out_specs=[vmem] * 4,
        out_shape=[jax.ShapeDtypeStruct((rows, width), jnp.float32)] * 4,
        scratch_shapes=[pltpu.VMEM((4, rows, width), jnp.float32)],
        compiler_params=pltpu.CompilerParams(vmem_limit_bytes=row_limit),
        cost_estimate=estimate(3),
        name="image_rows",
    )(place, scale, *own, *blocks, *layers, table, *inverse)


def move_columns(swaps, blocks, tables, move, forward, inverse):
    parts, rows, width = blocks[0].shape
    inner = parts * rows // 2
    return pl.pallas_call(
        x_kernel,
        in_specs=[smem] + [vmem] * (x_radix + 8),
        out_specs=[vmem] * x_radix,
        out_shape=[jax.ShapeDtypeStruct((parts, rows, width), jnp.float32)] * x_radix,
        scratch_shapes=[
            pltpu.VMEM((2 * x_radix, inner, width), jnp.bfloat16),
            pltpu.VMEM((2 * x_radix, inner, width), jnp.bfloat16),
            pltpu.VMEM((2 * x_radix, inner, width), jnp.float32),
        ],
        compiler_params=pltpu.CompilerParams(vmem_limit_bytes=column_limit),
        cost_estimate=estimate(6),
        name="move_columns",
    )(swaps, *blocks, *tables, move, *forward, *inverse)


def y_table(core, y_cols):
    k = (jnp.arange(y_radix, dtype=jnp.int32) ^ (4 * core))[:, None]
    r = jnp.arange(lanes, dtype=jnp.int32)[None, :]
    angles = 2.0 * math.pi / y_cols * (k * r % y_cols).astype(jnp.float32)
    return jnp.stack([jnp.cos(angles), -jnp.sin(angles)], axis=1)


def x_table(order, x_total):
    rows = x_total // x_radix
    low_bit, high_bit = order & 1, order >> 1
    slot = jnp.arange(x_radix, dtype=jnp.int32)
    k = jnp.where(slot % 2 == 1, slot ^ (2 * low_bit), slot)
    eighths = jnp.where(k % 2 == 1, 4 * high_bit, 0)
    turns = jnp.array([0, 6, 4, 2], jnp.int32)
    eighths = eighths + low_bit * turns[k]
    row = jnp.arange(rows, dtype=jnp.int32)[None, :]
    steps = (x_total // 8 * eighths[:, None] - k[:, None] * row) % x_total
    angles = 2.0 * math.pi / x_total * steps.astype(jnp.float32)
    table = jnp.stack([jnp.cos(angles), jnp.sin(angles)], axis=1)
    return jnp.broadcast_to(table[..., None], table.shape + (lanes,))


def cosine_sine(angles):
    half = 0.5 * angles
    square = half * half
    cosine, sine = 1.0 / math.factorial(12), -1.0 / math.factorial(11)
    for order in (10, 8, 6, 4, 2, 0):
        sign = -1.0 if order % 4 else 1.0
        cosine = cosine * square + sign / math.factorial(order)
        if order:
            sine = sine * square - sign / math.factorial(order - 1)
    sine = sine * half
    return 1.0 - 2.0 * sine * sine, 2.0 * sine * cosine


def half_table(rows):
    angles = -2.0 * np.pi / rows * np.arange(rows // 2)
    table = np.stack([np.cos(angles), np.sin(angles)]).astype(np.float32)
    return jnp.asarray(np.ascontiguousarray(np.broadcast_to(table[..., None], table.shape + (lanes,))))


def move_table(chunk, omega, polarity, core, x_total, y_total):
    step = jnp.arange(2 * x_radix, dtype=jnp.int32)[:, None]
    inner = jnp.arange(x_total // (2 * x_radix), dtype=jnp.int32)[None, :]
    x_waves = wave_number(step // 2 + x_radix * (2 * inner + step % 2), x_total)
    ky = jnp.arange(2, dtype=jnp.int32)[:, None] + 2 * chunk + y_radix // 2 * core
    inner = jnp.arange(lanes, dtype=jnp.int32)[None, :]
    y_waves = wave_number((ky + y_radix * inner).reshape(-1), y_total)
    lateral = x_waves[:, :, None] ** 2 + y_waves[None, None, :] ** 2
    kz_square = (omega * reference_slowness) ** 2 - lateral
    kz_root = jnp.sqrt(jnp.abs(kz_square))
    travels = kz_square >= 0.0
    amplitude = jnp.where(travels, 1.0, jnp.exp(-kz_root * depth_interval))
    amplitude = amplitude / (x_total * y_total)
    angles = jnp.where(travels, polarity * kz_root * depth_interval, 0.0)
    cosine, sine = cosine_sine(angles)
    return jnp.stack([amplitude * cosine, amplitude * sine], axis=1)


def zero_after(*others):
    corners = sum(other[(0,) * other.ndim] for other in others)
    return (corners * 0.0).astype(jnp.int32)


def per_device_fields(sizes, wavefields, slowness, freq_index):
    s, z, x, c = (lax.axis_index(axis) for axis in axes)
    rows, y_cols = wavefields.shape[3:]
    x_total = rows * sizes["gy"]
    place = jnp.stack([s, z, x, c]).astype(jnp.int32)

    def send(array, target):
        return lax.ppermute(array, axes, route(sizes, target))

    def to_core(array):
        return send(array, lambda s, z, x, c: (s, z, x, 1 - c))

    def to_partner(array):
        return send(array, lambda s, z, x, c: (s, z ^ 1, x, c))

    def to_partner_core(array):
        return send(array, lambda s, z, x, c: (s, z ^ 1, x, 1 - c))

    def to_freq(array):
        return send(array, lambda s, z, x, c: (s, z, 1 - x, c))

    def to_shot(array):
        return send(array, lambda s, z, x, c: (1 - s, z, x, c))

    def along_z(array, r):
        return send(array, lambda s, z, x, c: (s, z ^ r, x, c))

    row_forward = row_matrix(lanes, -1.0)
    row_inverse = row_matrix(lanes, 1.0)
    column_forward = column_matrix(rows // 2, -1.0)
    column_inverse = column_matrix(rows // 2, 1.0)

    width = y_cols // 8
    piece = lax.dynamic_slice_in_dim(slowness, (4 * s + 2 * x + c) * width, width, 2)
    pieces = [piece] + [along_z(piece, r) for r in (2, 3, 1)]

    def all_columns(late):
        stacked = jnp.stack([pieces[k] for k in (0, 3, 1, 2)], axis=1)
        mine = lax.dynamic_slice_in_dim(stacked, 2 * ((z // 2) ^ c) + late, 2, 1)
        theirs = to_core(
            lax.dynamic_slice_in_dim(stacked, 2 * ((z // 2) ^ (1 - c)) + late, 2, 1)
        )
        both = jnp.where(
            c == 0, jnp.concatenate([mine, theirs], 3), jnp.concatenate([theirs, mine], 3)
        )
        other = to_freq(both)
        pair = jnp.where(x == 0, jnp.stack([both, other]), jnp.stack([other, both]))
        return pair, to_shot(pair)

    y_steps = y_table(c, y_cols)
    spectra = origin_rows(wavefields[0], place, y_steps, row_forward)
    kept_is_odd = (z ^ c) % 2 == 1
    arrived = []
    for chunk in range(2):
        kept, crossed = spectra[chunk], to_core(spectra[2 + chunk])
        even = jnp.where(kept_is_odd, crossed, kept)
        odd = jnp.where(kept_is_odd, kept, crossed)
        far = along_z(even[1], 2)
        farthest = along_z(odd[1], 3)
        arrived.append([even[0], along_z(odd[0], 1), far, farthest])

    late = zero_after(arrived[0][1])
    layers = all_columns(late)

    z_late = z + late
    side = z_late % 2
    index = lax.dynamic_index_in_dim(freq_index, z_late // 2, 0, keepdims=False)
    omega = omega_unit * index.astype(jnp.float32)
    polarity = (2 * side - 1).astype(jnp.float32)
    order = 2 * c + side
    moves = [move_table(chunk, omega, polarity, c, x_total, y_cols) for chunk in range(2)]
    half = half_table(rows)
    table_z = x_table(z_late, x_total)
    table_order = x_table(order, x_total)
    scale = (polarity * omega).reshape(1)

    images = []
    blocks_in, order_in, table_in, hold = arrived, z, table_z, 0
    for depth_step in range(DEPTH):
        last = depth_step == DEPTH - 1
        swaps = jnp.stack([order_in & 1, order & 1]).astype(jnp.int32) + hold
        near, partner = [], []
        for chunk in range(2):
            out = move_columns(
                swaps, blocks_in[chunk], (table_in, table_order, half), moves[chunk],
                column_forward, column_inverse,
            )
            crossed = [to_core(out[2]), None if last else to_core(out[3])]
            near.append([[out[0], crossed[0]], [out[1], crossed[1]]])
            partner.append([to_partner(out[1]), to_partner_core(out[3])])

        def y_blocks(pairs):
            return [pairs[0][0], pairs[1][0], pairs[0][1], pairs[1][1]]

        own = y_blocks([near[0][0], near[1][0]])
        far_blocks = y_blocks(partner)
        if not last:
            turned = [None, None]
            waits = [zero_after(*partner[0]).astype(jnp.float32), 0.0]
            for slot in (1, 0):
                blocks = y_blocks([near[0][slot], near[1][slot]])
                turned[slot] = turn_rows(
                    slot == 0, (depth_step, slot), place, scale + waits[slot], blocks, layers, y_steps,
                    row_inverse, row_forward,
                )
            blocks_in = [
                [turned[0][k], turned[1][k], to_core(turned[0][2 + k]), to_core(turned[1][2 + k])]
                for k in range(2)
            ]
            hold = zero_after(partner[1][0])
            order_in, table_in = order, table_order
            own = [turned[0][4]]
        terms = image_rows(
            (depth_step, 0), place, scale, own, far_blocks, layers, y_steps, row_inverse
        )

        def gather(r):
            def target(s, z, x, c):
                quarter = (2 * x + z // 2) ^ r
                return s, 2 * c + z % 2, quarter // 2, quarter % 2

            return send(terms[r], target)

        images.append(sum(gather(r) for r in range(4)))
    return jnp.stack(images)


def solution(mesh):
    sizes = dict(mesh.shape)

    def per_device(wavefields, slowness, freq_index):
        if fits_one_field_per_chip(sizes, wavefields.shape):
            return per_device_fields(sizes, wavefields, slowness, freq_index)
        return per_device_pencils(wavefields, slowness, freq_index)

    placed = (P("fld", None, ("shot", "freq"), "gy", None), P(None, "gy", None), P("freq"))
    return jax.shard_map(
        per_device,
        mesh=mesh,
        in_specs=placed,
        out_specs=P("shot", "gy", ("freq", "fld")),
        check_vma=False,
    )
```
